128 devices in a mesh: gx: 8 (over y, core), gy: 16 (over z, x).
Axes of the slice: x: 4, y: 4, z: 4, core: 2. Of those that a mesh axis runs over, the one named last changes fastest.
Arguments:
- former_place_tile: int32 [32768], P(('gx', 'gy')), may hold values from -1 to 16383, as said below
- former_warmth: float32 [32768, 4096], P(('gx', 'gy')), may hold values from -6 to 6
- forcing_term: bfloat16 [32768, 4096], P(('gx', 'gy')), may hold values from -6 to 6
- diffusivity_map: bfloat16 [32768, 4096], P(('gx', 'gy')), may hold values from 0.5 to 8
- subdivision_depth: int32 [16384], P(('gx', 'gy')), may hold values from 0 to 2
- adjoining_tile: int32 [6, 16384], P(None, ('gx', 'gy')), may hold values from -1 to 16383, as said below
- adjoining_side: int32 [6, 16384], P(None, ('gx', 'gy')), may hold values from 0 to 5, as said below
- adjoining_rotation: int32 [6, 16384], P(None, ('gx', 'gy')), may hold values from 0 to 7, as said below
Outputs:
- new_temperature: float32 [16384, 4096], P(('gx', 'gy'))
The draws below stay inside these ranges and needn't reach their ends.
Inputs may be any that keep to these rules, and one draw needn't show every extreme that they name: `former_place_tile`: each block id 0 to 16383 stands in exactly one slot and every other slot holds -1. Block b belongs to owner b // 128, the device at that position along gx+gy. The 256 slots of one device hold at most 2 blocks of any one owner, and for every owner some device holds exactly 2 of its blocks. -1 marks a face without a link. Links are mutual: if adjoining_tile[f, b] = c and adjoining_side[f, b] = g then adjoining_tile[g, c] = b and adjoining_side[g, c] = f. The linked faces of a block name different blocks. A linked block belongs to the same owner or to the owner one step away along gx or along gy with the same index on the other axis; a block has at most one linked face toward any other owner, and every two owners adjacent in this way share exactly 32 links. `adjoining_side`: 0 where adjoining_tile is -1. `adjoining_rotation`: the two sides of a link carry inverse turns: where one side has o, the other has o if o < 4, else 4 + 2 (o % 2) + (o // 2) % 2. 0 where adjoining_tile is -1.
All inputs are finite; a program needn't handle non-finite values.
Results may differ from the reference program's by a relative error of at most 0.00045.
Values may be sent and summed in bfloat16 or wider, within the bound.
A program may use at most 192 MiB of HBM per device.

```python
import math
import jax
import jax.numpy as jnp

B = 16
VOXELS_IN_TILE = 4096
BRICK_XY = 4
BRICK_Z = 8
SWEEPS = 3
BLK_DEV = 128
PAIR_CAP = 2
SLOT_DEV = 256
BLOCKS = 16384
PLACES_OVERALL = 32768
EXTENT_X = 32
EXTENT_Y = 64


def draw_former_place_tile(key, part):
    machines = SLOT_DEV // PAIR_CAP
    candidates_count = PAIR_CAP * machines
    owners = jnp.arange(machines, dtype=jnp.int32)

    def pick_for(owner_id):
        scores = jax.random.permutation(jax.random.fold_in(key, owner_id), candidates_count).astype(jnp.int32)
        candidate = jnp.arange(candidates_count, dtype=jnp.int32)
        forced = candidate // PAIR_CAP == (owner_id + 1) % machines
        scores = jnp.where(forced, -1 - candidate % PAIR_CAP, scores)
        return jnp.argsort(scores)[:BLK_DEV].astype(jnp.int32)
    chosen = jax.vmap(pick_for)(owners)
    holder = chosen // PAIR_CAP
    copy_index = chosen % PAIR_CAP
    spot = holder * SLOT_DEV + owners[:, None] * PAIR_CAP + copy_index
    block_ids = owners[:, None] * BLK_DEV + jnp.arange(BLK_DEV, dtype=jnp.int32)[None, :]
    table = jnp.full((machines * SLOT_DEV,), -1, jnp.int32).at[spot.reshape(-1)].set(block_ids.reshape(-1))

    def shuffle(device_id):
        return jax.random.permutation(jax.random.fold_in(jax.random.fold_in(key, 7777), device_id), SLOT_DEV).astype(jnp.int32)
    orders = jax.vmap(shuffle)(owners)
    return jnp.take_along_axis(table.reshape(machines, SLOT_DEV), orders, axis=1).reshape(-1)


def invert_turn(orient):
    return jnp.where(orient >= 4, 4 + 2 * (orient % 2) + orient // 2 % 2, orient)


def neighbour_tables(key):
    lines_y = EXTENT_Y // BRICK_XY
    total_blocks = BLOCKS
    block_ids = jnp.arange(total_blocks, dtype=jnp.int32)
    owner_ids = block_ids // BLK_DEV
    inside = block_ids % BLK_DEV
    coord_x = owner_ids // lines_y * BRICK_XY + inside // (BRICK_XY * BRICK_Z)
    coord_y = owner_ids % lines_y * BRICK_XY + inside // BRICK_Z % BRICK_XY
    coord_z = inside % BRICK_Z

    def block_at(at_x, at_y, at_z):
        holder = at_x // BRICK_XY * lines_y + at_y // BRICK_XY
        within = (at_x % BRICK_XY * BRICK_XY + at_y % BRICK_XY) * BRICK_Z + at_z
        return holder * BLK_DEV + within
    void_gaps = jax.random.randint(jax.random.fold_in(key, 11), (total_blocks,), 0, 8) == 0
    pair_turns = jax.random.randint(jax.random.fold_in(key, 12), (total_blocks, 3), 0, 8).astype(jnp.int32)

    def label_perm(sub_key):
        return jax.random.permutation(sub_key, 6)
    labels = jax.vmap(label_perm)(jax.random.split(jax.random.fold_in(key, 13), total_blocks)).astype(jnp.int32)
    offsets = [(-1, 0, 0), (1, 0, 0), (0, -1, 0), (0, 1, 0), (0, 0, -1), (0, 0, 1)]
    side_block = []
    side_face = []
    side_turn = []
    for side_index in range(6):
        step_x, step_y, step_z = offsets[side_index]
        next_x = coord_x + step_x
        next_y = coord_y + step_y
        next_z = coord_z + step_z
        present = (next_x >= 0) & (next_x < EXTENT_X) & (next_y >= 0) & (next_y < EXTENT_Y) & (next_z >= 0) & (next_z < BRICK_Z)
        across = block_at(jnp.clip(next_x, 0, EXTENT_X - 1), jnp.clip(next_y, 0, EXTENT_Y - 1), jnp.clip(next_z, 0, BRICK_Z - 1))
        if side_index == 4:
            present = present & jnp.logical_not(void_gaps[across])
        if side_index == 5:
            present = present & jnp.logical_not(void_gaps)
        axis_index = side_index // 2
        if side_index % 2 == 1:
            turn_here = pair_turns[:, axis_index]
        else:
            turn_here = invert_turn(pair_turns[across, axis_index])
        face_there = labels[across, side_index ^ 1]
        side_block.append(jnp.where(present, across, -1))
        side_face.append(jnp.where(present, face_there, 0))
        side_turn.append(jnp.where(present, turn_here, 0))
    rows_index = labels.T
    cols_index = jnp.broadcast_to(block_ids[None, :], (6, total_blocks))
    blank = jnp.zeros((6, total_blocks), jnp.int32)
    table_block = blank.at[rows_index, cols_index].set(jnp.stack(side_block).astype(jnp.int32))
    table_face = blank.at[rows_index, cols_index].set(jnp.stack(side_face).astype(jnp.int32))
    table_turn = blank.at[rows_index, cols_index].set(jnp.stack(side_turn).astype(jnp.int32))
    return (table_block, table_face, table_turn)


def draw_adjoining_tile(key, part):
    return neighbour_tables(key)[0]


def draw_adjoining_side(key, part):
    return neighbour_tables(key)[1]


def draw_adjoining_rotation(key, part):
    return neighbour_tables(key)[2]


def with_ends(array, stream_key, smallest, high):
    longest = array.shape.index(max(array.shape))
    spots = []
    for shift in (0, 1):
        where = [jax.random.randint(jax.random.fold_in(stream_key, axis), (), 0, length) for axis, length in enumerate(array.shape)]
        where[longest] = (where[longest] + shift) % array.shape[longest]
        spots.append(tuple(where))
    return array.at[spots[0]].set(smallest).at[spots[1]].set(high)


def block_levels(stream_key, shape, pieces, low, top_value):
    gain = 1.0
    for position, parts in pieces:
        draws = jax.random.uniform(jax.random.fold_in(jax.random.fold_in(stream_key, 6), position), (parts,), jnp.float32, low / len(pieces), top_value / len(pieces))
        gain = gain * jnp.repeat(jnp.exp(draws), shape[position] // parts).reshape((-1,) + (1,) * (len(shape) - 1 - position))
    return gain


def scatter_about(key, extent, scale, reach, cuts=(), held_as=jnp.bfloat16):
    level = block_levels(key, extent, cuts, -0.22, 0.18) if cuts else 1.0
    entries = jax.random.normal(key, extent, jnp.float32) * scale * level
    return jnp.minimum(jnp.maximum(entries, -reach), reach).astype(held_as)


def setup_inputs(seed: int = 0) -> dict:
    key_list = jax.random.split(jax.random.key(seed), 9)
    return {
        "former_place_tile": draw_former_place_tile(jax.random.fold_in(key_list[8], 71), 0),
        "former_warmth": scatter_about(key_list[1], (PLACES_OVERALL, VOXELS_IN_TILE), 1.0, 6.0, ((0, 128),), jnp.float32),
        "forcing_term": scatter_about(key_list[2], (PLACES_OVERALL, VOXELS_IN_TILE), 1.0, 6.0, ((0, 128),)),
        "diffusivity_map": jnp.clip(jnp.exp(math.log(8.0) - 2.7725887 * jax.random.uniform(key_list[3], (PLACES_OVERALL, VOXELS_IN_TILE), jnp.float32) ** block_levels(key_list[3], (PLACES_OVERALL, VOXELS_IN_TILE), ((0, 128),), -0.2, 0.2)), 0.5, 8.0).astype(jnp.bfloat16),
        "subdivision_depth": with_ends(jax.random.randint(key_list[4], (BLOCKS,), 0, 3), jax.random.fold_in(key_list[4], 1), 0, 2).astype(jnp.int32),
        "adjoining_tile": draw_adjoining_tile(jax.random.fold_in(key_list[8], 71), 0),
        "adjoining_side": draw_adjoining_side(jax.random.fold_in(key_list[8], 71), 0),
        "adjoining_rotation": draw_adjoining_rotation(jax.random.fold_in(key_list[8], 71), 0),
    }


MASS_TERM = 4.0
LOWER_BOUND = 0.25
UPPER_BOUND = 2.0


def harmonic(near_side, far_side):
    return 2.0 * near_side * far_side / (near_side + far_side)


def face_planes(volume):
    return jnp.stack([volume[:, 0], volume[:, -1], volume[:, :, 0], volume[:, :, -1], volume[:, :, :, 0], volume[:, :, :, -1]])


def place_faces(planes, tile_width):
    summed = jnp.zeros(tile_width, jnp.float32)
    summed = summed.at[:, 0].add(planes[0])
    summed = summed.at[:, -1].add(planes[1])
    summed = summed.at[:, :, 0].add(planes[2])
    summed = summed.at[:, :, -1].add(planes[3])
    summed = summed.at[:, :, :, 0].add(planes[4])
    summed = summed.at[:, :, :, -1].add(planes[5])
    return summed


def rotate_planes(planes, orient):
    swap_axes = (orient // 4 == 1)[..., None, None]
    flip_rows = (orient % 2 == 1)[..., None, None]
    flip_cols = ((orient // 2) % 2 == 1)[..., None, None]
    turned = jnp.where(swap_axes, jnp.swapaxes(planes, -1, -2), planes)
    turned = jnp.where(flip_rows, jnp.flip(turned, -2), turned)
    return jnp.where(flip_cols, jnp.flip(turned, -1), turned)


def couplings(volume):
    along_first = harmonic(volume[:, 1:], volume[:, :-1])
    along_second = harmonic(volume[:, :, 1:], volume[:, :, :-1])
    along_third = harmonic(volume[:, :, :, 1:], volume[:, :, :, :-1])
    return along_first, along_second, along_third


def inner_sum(values, link_sets):
    along_first, along_second, along_third = link_sets
    summed = jnp.zeros(values.shape, jnp.float32)
    summed = summed.at[:, 1:].add(along_first * values[:, :-1])
    summed = summed.at[:, :-1].add(along_first * values[:, 1:])
    summed = summed.at[:, :, 1:].add(along_second * values[:, :, :-1])
    summed = summed.at[:, :, :-1].add(along_second * values[:, :, 1:])
    summed = summed.at[:, :, :, 1:].add(along_third * values[:, :, :, :-1])
    summed = summed.at[:, :, :, :-1].add(along_third * values[:, :, :, 1:])
    return summed


def residual_of(values, right_side, diagonal, link_sets, face_links, neighbour_fn):
    pulled = inner_sum(values, link_sets) + place_faces(face_links * neighbour_fn(values), values.shape)
    return (right_side - (diagonal * values - pulled)) / diagonal


def chebyshev(start, right_side, diagonal, link_sets, face_links, neighbour_fn):
    centre = 0.5 * (UPPER_BOUND + LOWER_BOUND)
    half_width = 0.5 * (UPPER_BOUND - LOWER_BOUND)
    relative = centre / half_width
    ratio_now = 1.0 / relative
    update = residual_of(start, right_side, diagonal, link_sets, face_links, neighbour_fn) / centre
    iterate = start + update
    for repeat in range(SWEEPS - 1):
        ratio_next = 1.0 / (2.0 * relative - ratio_now)
        update = ratio_next * ratio_now * update + (2.0 * ratio_next / half_width) * residual_of(iterate, right_side, diagonal, link_sets, face_links, neighbour_fn)
        iterate = iterate + update
        ratio_now = ratio_next
    return iterate


def reference(former_place_tile, former_warmth, forcing_term, diffusivity_map, subdivision_depth, adjoining_tile, adjoining_side, adjoining_rotation):
    blocks = subdivision_depth.shape[0]
    target = jnp.where(former_place_tile >= 0, former_place_tile, blocks).astype(jnp.int32)
    arriving_place = jnp.zeros((blocks,), jnp.int32).at[target].set(jnp.arange(former_place_tile.shape[0], dtype=jnp.int32), mode="drop")
    tile_width = (blocks, B, B, B)
    warmth_grid = former_warmth[arriving_place].reshape(tile_width)
    heat_source = forcing_term[arriving_place].astype(jnp.float32).reshape(tile_width)
    kappa_cell = diffusivity_map[arriving_place].astype(jnp.float32).reshape(tile_width)
    level_scale = jnp.left_shift(jnp.ones_like(subdivision_depth), 2 * subdivision_depth).astype(jnp.float32)
    conduct = kappa_cell * level_scale[:, None, None, None]
    link_sets = couplings(conduct)
    linked = adjoining_tile >= 0
    face_rows = jnp.where(linked, adjoining_side * blocks + adjoining_tile, 0).astype(jnp.int32)

    def neighbour_fn(volume):
        flat_planes = face_planes(volume).reshape(6 * blocks, B, B)
        return rotate_planes(flat_planes[face_rows], adjoining_rotation)

    face_links = jnp.where(linked[..., None, None], harmonic(face_planes(conduct), neighbour_fn(conduct)), 0.0)
    diagonal = MASS_TERM + inner_sum(jnp.ones(tile_width, jnp.float32), link_sets) + place_faces(face_links, tile_width)
    right_side = MASS_TERM * (warmth_grid + heat_source)
    iterate = chebyshev(warmth_grid, right_side, diagonal, link_sets, face_links, neighbour_fn)
    return iterate.reshape(blocks, VOXELS_IN_TILE)
```

```python
import functools

import jax
import jax.numpy as jnp
from jax import lax
from jax.experimental import pallas as pl
from jax.experimental.pallas import tpu as pltpu
from jax.sharding import PartitionSpec as P

B = 16
PLANE = B * B
CELLS = B * B * B
SWEEPS = 3
MASS_TERM = 4.0
LOWER_BOUND = 0.25
UPPER_BOUND = 2.0
CHUNK = 128
PAD = PLANE
LEVELS = 32767.0
F32 = jnp.float32
BF16 = jnp.bfloat16
I32 = jnp.int32
MESH = pl.DeviceIdType.MESH


def dot(a, b):
    return jnp.dot(a, b, preferred_element_type=F32)


def plane_rows(ref, base, face):
    if face == 0:
        return ref[pl.ds(base, PLANE), :]
    if face == 1:
        return ref[pl.ds(base + 15 * PLANE, PLANE), :]
    if face in (2, 3):
        first = base + (0 if face == 2 else PLANE - B)
        return jnp.concatenate([ref[pl.ds(first + PLANE * u, B), :] for u in range(B)], axis=0)
    return ref[pl.ds(base + (0 if face == 4 else B - 1), PLANE, stride=B), :]


def crossed_groups(ref, base, face):
    if face < 2:
        first, step, stride = base + 15 * PLANE * face, 1, B
    elif face < 4:
        first, step, stride = base + (PLANE - B) * (face - 2), 1, PLANE
    else:
        first, step, stride = base + (B - 1) * (face - 4), B, PLANE
    return [ref[pl.ds(first + step * v, B, stride=stride), :] for v in range(B)]


def face_update(ref, base, face, added):
    if face < 2:
        at = pl.ds(base + 15 * PLANE * face, PLANE)
        ref[at, :] = ref[at, :] + added
    elif face < 4:
        first = base + (PLANE - B) * (face - 2)
        for u in range(B):
            at = pl.ds(first + PLANE * u, B)
            ref[at, :] = ref[at, :] + added[u * B : (u + 1) * B]
    else:
        at = pl.ds(base + (B - 1) * (face - 4), PLANE, stride=B)
        ref[at, :] = ref[at, :] + added


def harmonic(p, q):
    return 2.0 * p * q / (p + q)


def kernel(
    devices,
    minor,
    place_ref,
    depth_ref,
    tile_ref,
    side_ref,
    turn_ref,
    warm_hbm,
    heat_hbm,
    kappa_hbm,
    out_ref,
    warm_in,
    heat_in,
    kappa_in,
    meta_out,
    meta_got,
    words_out,
    words_got,
    onehot,
    settle,
    conduct,
    link_i,
    link_j,
    link_k,
    right,
    inverse,
    field_a,
    field_b,
    change,
    gather,
    choose,
    turned,
    high,
    low,
    leaving,
    arriving,
    face_link,
    load_sem,
    meta_sems,
    send_sems,
    recv_sems,
    face_send,
    face_recv,
):
    major = devices // minor
    gx = lax.axis_index("gx")
    gy = lax.axis_index("gy")
    me = gx * minor + gy
    slots = place_ref.shape[1]
    lanes = 128
    barrier = pltpu.get_barrier_semaphore()

    def peer(t):
        p = lax.rem(me + t, devices)
        return p, (p // minor, lax.rem(p, minor))

    def greet(t, carry):
        pl.semaphore_signal(barrier, inc=1, device_id=peer(t)[1], device_id_type=MESH)
        return carry

    loads = [
        pltpu.make_async_copy(kappa_hbm, kappa_in, load_sem.at[0]),
        pltpu.make_async_copy(warm_hbm, warm_in, load_sem.at[1]),
        pltpu.make_async_copy(heat_hbm, heat_in, load_sem.at[2]),
    ]
    for copy in loads:
        copy.start()
    lax.fori_loop(1, devices, greet, 0)

    place_row = place_ref[...].astype(F32)
    row_id = lax.broadcasted_iota(I32, (slots, slots), 0)
    col_id = lax.broadcasted_iota(I32, (slots, slots), 1)
    place_wide = jnp.broadcast_to(place_row, (slots, slots))
    place_col = jnp.sum(jnp.where(row_id == col_id, place_wide, 0.0), axis=1, keepdims=True)
    owner_row = jnp.floor(place_wide * (1.0 / lanes))
    owner_col = jnp.floor(place_col * (1.0 / lanes))
    again = jnp.sum(
        jnp.where((owner_row == owner_col) & (row_id < col_id), 1.0, 0.0), axis=0, keepdims=True
    )
    row_at = jnp.where(place_row >= 0.0, again * devices + owner_row[:1], -1.0)
    onehot[...] = jnp.where(row_id.astype(F32) == row_at, 1.0, 0.0).astype(BF16)
    tag_col = jnp.where(place_col >= 0.0, place_col - owner_col * lanes + 1.0, 0.0)
    tags = dot(onehot[...], jnp.broadcast_to(tag_col, (slots, lanes)).astype(BF16))

    def put_words(field, t, words):
        for s in range(2):
            words_out[field, pl.ds(s * B + t, devices, stride=2 * B), :] = words[
                s * devices : (s + 1) * devices
            ]

    def send_field(field):
        def one(t, carry):
            p, where = peer(t)
            pltpu.make_async_remote_copy(
                words_out.at[field, pl.ds(pl.multiple_of(p * 2 * B, 2 * B), 2 * B)],
                words_got.at[field, pl.ds(pl.multiple_of(me * 2 * B, 2 * B), 2 * B)],
                send_sems.at[field],
                recv_sems.at[field],
                device_id=where,
                device_id_type=MESH,
            ).start()
            return carry

        lax.fori_loop(1, devices, one, 0)
        mine = pl.ds(pl.multiple_of(me * 2 * B, 2 * B), 2 * B)
        words_got[field, mine, :] = words_out[field, mine, :]

    loads[0].wait()

    def pack_kappa(t, carry):
        both = dot(onehot[...], kappa_in[:, pl.ds(pl.multiple_of(t * PLANE, PLANE), PLANE)])
        ints = (both * 256.0).astype(I32)
        put_words(0, t, ints[:, :lanes] + ints[:, lanes:] * 65536)
        return carry

    lax.fori_loop(0, B, pack_kappa, 0)
    pl.semaphore_wait(barrier, devices - 1)
    send_field(0)

    loads[1].wait()
    loads[2].wait()

    def scale_of(ref):
        def one(t, best):
            at = pl.ds(pl.multiple_of(t * lanes, lanes), lanes)
            return jnp.maximum(best, jnp.abs(ref[:, at].astype(F32)))

        best = lax.fori_loop(0, CELLS // lanes, one, jnp.zeros((slots, lanes), F32))
        largest = jnp.maximum(jnp.max(best, axis=1, keepdims=True) * 1.005, 1e-30)
        return dot(onehot[...], jnp.broadcast_to(largest, (slots, lanes)).astype(BF16))

    warm_scale = scale_of(warm_in)
    heat_scale = scale_of(heat_in)
    lane_id = lax.broadcasted_iota(I32, (devices, lanes), 1)
    meta = jnp.zeros((devices, lanes), F32)
    for n, part in enumerate((tags, warm_scale, heat_scale)):
        for s in range(2):
            meta = jnp.where(lane_id == 2 * n + s, part[s * devices : (s + 1) * devices], meta)
    meta_out[...] = meta.reshape(devices, 1, lanes)
    meta_got[pl.ds(me, 1)] = meta_out[pl.ds(me, 1)]

    def send_meta(t, carry):
        p, where = peer(t)
        pltpu.make_async_remote_copy(
            meta_out.at[p],
            meta_got.at[me],
            meta_sems.at[0],
            meta_sems.at[1],
            device_id=where,
            device_id_type=MESH,
        ).start()
        return carry

    lax.fori_loop(1, devices, send_meta, 0)

    def factor(scale):
        return jnp.where(scale > 0.0, LEVELS / jnp.maximum(scale, 1e-31), 0.0)

    warm_factor = factor(warm_scale)
    heat_factor = factor(heat_scale)

    def words_of(both, scale):
        ints = [jnp.round(both[:, c * lanes : (c + 1) * lanes] * scale).astype(I32) for c in (0, 1)]
        return ints[0] + ints[1] * 65536

    def pack_warm(t, carry):
        value = warm_in[:, pl.ds(pl.multiple_of(t * PLANE, PLANE), PLANE)]
        top = value.astype(BF16)
        rest = (value - top.astype(F32)).astype(BF16)
        both = dot(onehot[...], top) + dot(onehot[...], rest)
        put_words(1, t, words_of(both, warm_factor))
        return carry

    lax.fori_loop(0, B, pack_warm, 0)
    send_field(1)

    def pack_heat(t, carry):
        both = dot(onehot[...], heat_in[:, pl.ds(pl.multiple_of(t * PLANE, PLANE), PLANE)])
        put_words(2, t, words_of(both, heat_factor))
        return carry

    lax.fori_loop(0, B, pack_heat, 0)
    send_field(2)

    swaps, flip_rows, flip_cols, linked = [], [], [], []
    ways = []
    sources = []
    for f in range(6):
        tile = tile_ref[f : f + 1, :]
        turn = turn_ref[f : f + 1, :]
        owner = tile >> 7
        inside = tile & 127
        live = tile >= 0
        way = jnp.where(
            owner == me - minor,
            0,
            jnp.where(owner == me + minor, 1, jnp.where(owner == me - 1, 2, 3)),
        )
        way = jnp.where(owner == me, -1, way)
        way = jnp.where(live, way, -2)
        ways.append(way)
        source = jnp.where(way == -1, side_ref[f : f + 1, :] * lanes + inside, 6 * lanes + way * lanes + inside)
        sources.append(jnp.where(live, source, -1))
        swap = turn >> 2
        bit_0 = turn & 1
        bit_1 = (turn >> 1) & 1
        swaps.append(jnp.broadcast_to(swap, (B, lanes)) > 0)
        flip_rows.append(jnp.broadcast_to(jnp.where(swap > 0, bit_1, bit_0), (B, lanes)) > 0)
        flip_cols.append(jnp.broadcast_to(jnp.where(swap > 0, bit_0, bit_1), (B, lanes)) > 0)
        linked.append(jnp.broadcast_to(tile, (PLANE, lanes)) >= 0)
    square = lax.broadcasted_iota(I32, (lanes, lanes), 0)
    across = lax.broadcasted_iota(I32, (lanes, lanes), 1)
    for f in range(6):
        at = pl.ds(f * lanes, lanes)
        for n in range(10):
            gather[pl.ds(n * lanes, lanes), at] = jnp.where(
                square + n * lanes == sources[f], 1.0, 0.0
            ).astype(BF16)
        for d in range(4):
            choose[at, pl.ds(d * lanes, lanes)] = jnp.where(
                (square == across) & (ways[f] == d), 1.0, 0.0
            ).astype(BF16)
    for ref in (conduct, link_i, link_j, link_k, field_a, field_b):
        fill = jnp.full((PAD, lanes), 1.0 if ref is conduct else 0.0, F32)
        ref[pl.ds(0, PAD), :] = fill
        ref[pl.ds(PAD + CELLS, PAD), :] = fill

    neighbours = (
        (lax.rem(gx + major - 1, major), gy),
        (lax.rem(gx + 1, major), gy),
        (gx, lax.rem(gy + minor - 1, minor)),
        (gx, lax.rem(gy + 1, minor)),
    )

    def face_copies(round_):
        return [
            pltpu.make_async_remote_copy(
                leaving.at[round_, d],
                arriving.at[round_, d ^ 1],
                face_send.at[round_, d],
                face_recv.at[round_, d ^ 1],
                device_id=neighbours[d],
                device_id_type=MESH,
            )
            for d in range(4)
        ]

    def start_faces(ref, round_):
        for f in range(6):
            plain = plane_rows(ref, PAD, f)
            crossed = crossed_groups(ref, PAD, f)
            laid = [
                jnp.where(swaps[f], plain[c * B : (c + 1) * B], crossed[c]) for c in range(B)
            ]
            for c in range(B):
                turned[pl.ds(f * PLANE + c * B, B), :] = jnp.where(
                    flip_cols[f], laid[B - 1 - c], laid[c]
                )
        for f in range(6):
            back = [turned[pl.ds(f * PLANE + r, B, stride=B), :] for r in range(B)]
            plane = jnp.concatenate(
                [jnp.where(flip_rows[f], back[B - 1 - r], back[r]) for r in range(B)], axis=0
            )
            top = plane.astype(BF16)
            at = pl.ds(f * lanes, lanes)
            high[:, at] = top
            if round_ > 0:
                low[:, at] = (plane - top.astype(F32)).astype(BF16)
        for d in range(4):
            leaving[round_, d] = dot(high[...], choose[:, pl.ds(d * lanes, lanes)]).astype(BF16)
        for copy in face_copies(round_):
            copy.start()

    def finish_faces(round_, use):
        for copy in face_copies(round_):
            copy.wait()
        for pair in range(3):
            at = pl.ds(pair * 2 * lanes, 2 * lanes)
            planes = dot(high[...], gather[pl.ds(0, 6 * lanes), at])
            if round_ > 0:
                planes = planes + dot(low[...], gather[pl.ds(0, 6 * lanes), at])
            for d in range(4):
                planes = planes + dot(arriving[round_, d], gather[pl.ds((6 + d) * lanes, lanes), at])
            use(2 * pair, planes[:, :lanes])
            use(2 * pair + 1, planes[:, lanes:])

    def arrived(sems, sem, buffer):
        pltpu.make_async_copy(buffer, buffer, sems.at[sem]).wait()

    def all_but_mine(field):
        return words_got.at[field, pl.ds(0, (devices - 1) * 2 * B)]

    arrived(meta_sems, 1, meta_got.at[pl.ds(0, devices - 1)])
    meta = meta_got[...].reshape(devices, lanes)
    spread = [
        jnp.concatenate(
            [jnp.broadcast_to(meta[:, 2 * n + s : 2 * n + s + 1], (devices, lanes)) for s in range(2)],
            axis=0,
        )
        for n in range(3)
    ]
    block_id = lax.broadcasted_iota(I32, (2 * devices, lanes), 1).astype(F32)
    chosen = jnp.where(spread[0] == block_id + 1.0, 1.0, 0.0)
    warm_unit = jnp.sum(chosen * spread[1], axis=0, keepdims=True) * (1.0 / LEVELS)
    heat_unit = jnp.sum(chosen * spread[2], axis=0, keepdims=True) * (1.0 / LEVELS)
    by_block = chosen.T
    settle[:, : 2 * devices] = (by_block * 256.0).astype(BF16)
    settle[:, 2 * devices :] = by_block.astype(BF16)

    def words_at(field, t):
        words = jnp.concatenate(
            [words_got[field, pl.ds(s * B + t, devices, stride=2 * B), :] for s in range(2)], axis=0
        )
        second = (words + 32768) >> 16
        first = words - second * 65536
        return jnp.concatenate([first, second], axis=1)

    def placed_16(field, t):
        ints = words_at(field, t)
        top = ints >> 8
        rest = ints & 255
        parts = jnp.concatenate([top.astype(F32).astype(BF16), rest.astype(F32).astype(BF16)], axis=0)
        return dot(settle[...], parts).T

    depth = depth_ref[...]
    level = jnp.where(depth == 0, 1.0, jnp.where(depth == 1, 4.0, 16.0)) * (1.0 / 256.0)

    def rows_of(t):
        return pl.ds(pl.multiple_of(PAD + t * PLANE, PLANE), PLANE)

    arrived(recv_sems, 0, all_but_mine(0))

    def place_kappa(t, carry):
        ints = words_at(0, t).astype(F32).astype(BF16)
        conduct[rows_of(t), :] = dot(settle[:, 2 * devices :], ints).T * level
        return carry

    lax.fori_loop(0, B, place_kappa, 0)
    start_faces(conduct, 0)

    row_in = lax.broadcasted_iota(I32, (CHUNK, lanes), 0)
    inner_k = (row_in & (B - 1)) < B - 1
    chunks = CELLS // CHUNK

    def at_chunk(n, shift=0):
        return pl.ds(pl.multiple_of(PAD + n * CHUNK, CHUNK) + shift, CHUNK)

    def make_links(n, carry):
        here = conduct[at_chunk(n), :]
        row = row_in + n * CHUNK
        link_i[at_chunk(n), :] = jnp.where(
            row < CELLS - PLANE, harmonic(here, conduct[at_chunk(n, PLANE), :]), 0.0
        )
        link_j[at_chunk(n), :] = jnp.where(
            (row & (PLANE - 1)) < PLANE - B, harmonic(here, conduct[at_chunk(n, B), :]), 0.0
        )
        link_k[at_chunk(n), :] = jnp.where(inner_k, harmonic(here, conduct[at_chunk(n, 1), :]), 0.0)
        return carry

    lax.fori_loop(0, chunks, make_links, 0)

    def add_links(n, carry):
        inverse[at_chunk(n), :] = (
            MASS_TERM
            + link_i[at_chunk(n), :]
            + link_i[at_chunk(n, -PLANE), :]
            + link_j[at_chunk(n), :]
            + link_j[at_chunk(n, -B), :]
            + link_k[at_chunk(n), :]
            + link_k[at_chunk(n, -1), :]
        )
        return carry

    lax.fori_loop(0, chunks, add_links, 0)

    def make_face_links(f, planes):
        links = jnp.where(
            linked[f], harmonic(plane_rows(conduct, PAD, f), jnp.where(linked[f], planes, 1.0)), 0.0
        )
        face_link[f] = links
        face_update(inverse, PAD, f, links)

    finish_faces(0, make_face_links)

    def invert(n, carry):
        inverse[at_chunk(n), :] = 1.0 / inverse[at_chunk(n), :]
        return carry

    lax.fori_loop(0, chunks, invert, 0)
    for f in range(6):
        face_link[f] = face_link[f] * plane_rows(inverse, PAD, f)

    arrived(recv_sems, 1, all_but_mine(1))

    def place_warm(t, carry):
        field_a[rows_of(t), :] = placed_16(1, t) * warm_unit
        return carry

    lax.fori_loop(0, B, place_warm, 0)
    start_faces(field_a, 1)

    arrived(recv_sems, 2, all_but_mine(2))

    def place_heat(t, carry):
        right[rows_of(t), :] = MASS_TERM * (field_a[rows_of(t), :] + placed_16(2, t) * heat_unit)
        return carry

    lax.fori_loop(0, B, place_heat, 0)

    centre = 0.5 * (UPPER_BOUND + LOWER_BOUND)
    half_width = 0.5 * (UPPER_BOUND - LOWER_BOUND)
    relative = centre / half_width
    ratio = 1.0 / relative
    now, then = field_a, field_b
    for sweep in range(SWEEPS):
        if sweep == 0:
            keep, gain = 0.0, 1.0 / centre
        else:
            ratio_next = 1.0 / (2.0 * relative - ratio)
            keep, gain = ratio_next * ratio, 2.0 * ratio_next / half_width
            ratio = ratio_next
            start_faces(now, sweep + 1)

        def relax(n, carry, now=now, then=then, keep=keep, gain=gain, sweep=sweep):
            here = now[at_chunk(n), :]
            pulled = (
                right[at_chunk(n), :]
                + link_i[at_chunk(n), :] * now[at_chunk(n, PLANE), :]
                + link_i[at_chunk(n, -PLANE), :] * now[at_chunk(n, -PLANE), :]
                + link_j[at_chunk(n), :] * now[at_chunk(n, B), :]
                + link_j[at_chunk(n, -B), :] * now[at_chunk(n, -B), :]
                + link_k[at_chunk(n), :] * now[at_chunk(n, 1), :]
                + link_k[at_chunk(n, -1), :] * now[at_chunk(n, -1), :]
            )
            step = gain * (pulled * inverse[at_chunk(n), :] - here)
            if sweep > 0:
                step = step + keep * change[at_chunk(n), :]
            if sweep < SWEEPS - 1:
                change[at_chunk(n), :] = step
            then[at_chunk(n), :] = here + step
            return carry

        lax.fori_loop(0, chunks, relax, 0)

        def add_faces(f, planes, then=then, gain=gain, sweep=sweep):
            added = gain * face_link[f] * planes
            face_update(then, PAD, f, added)
            if sweep < SWEEPS - 1:
                face_update(change, PAD, f, added)

        finish_faces(sweep + 1, add_faces)
        now, then = then, now

    def write_out(t, carry):
        out_ref[:, pl.ds(pl.multiple_of(t * PLANE, PLANE), PLANE)] = now[rows_of(t), :].T
        return carry

    lax.fori_loop(0, B, write_out, 0)

    arrived(meta_sems, 0, meta_out.at[pl.ds(0, devices - 1)])
    for field in range(3):
        arrived(send_sems, field, words_out.at[field, pl.ds(0, (devices - 1) * 2 * B)])


def local(place, warmth, forcing, kappa, depth, tile, side, turn, devices, minor):
    slots = place.shape[0]
    blocks = depth.shape[0]
    lanes = 128
    tall = CELLS + 2 * PAD
    vmem = pl.BlockSpec(memory_space=pltpu.VMEM)
    hbm = pl.BlockSpec(memory_space=pl.ANY)
    tall_field = pltpu.VMEM((tall, lanes), F32)
    return pl.pallas_call(
        functools.partial(kernel, devices, minor),
        out_shape=jax.ShapeDtypeStruct((blocks, CELLS), F32),
        in_specs=[vmem] * 5 + [hbm] * 3,
        out_specs=vmem,
        scratch_shapes=[
            pltpu.VMEM((slots, CELLS), F32),
            pltpu.VMEM((slots, CELLS), BF16),
            pltpu.VMEM((slots, CELLS), BF16),
            pltpu.VMEM((devices, 1, lanes), F32),
            pltpu.VMEM((devices, 1, lanes), F32),
            pltpu.VMEM((3, devices * 2 * B, lanes), I32),
            pltpu.VMEM((3, devices * 2 * B, lanes), I32),
            pltpu.VMEM((slots, slots), BF16),
            pltpu.VMEM((blocks, 4 * devices), BF16),
            tall_field,
            tall_field,
            tall_field,
            tall_field,
            tall_field,
            tall_field,
            tall_field,
            tall_field,
            tall_field,
            pltpu.VMEM((10 * lanes, 6 * lanes), BF16),
            pltpu.VMEM((6 * lanes, 4 * lanes), BF16),
            pltpu.VMEM((6 * PLANE, lanes), F32),
            pltpu.VMEM((PLANE, 6 * lanes), BF16),
            pltpu.VMEM((PLANE, 6 * lanes), BF16),
            pltpu.VMEM((SWEEPS + 1, 4, PLANE, lanes), BF16),
            pltpu.VMEM((SWEEPS + 1, 4, PLANE, lanes), BF16),
            pltpu.VMEM((6, PLANE, lanes), F32),
            pltpu.SemaphoreType.DMA((3,)),
            pltpu.SemaphoreType.DMA((2,)),
            pltpu.SemaphoreType.DMA((3,)),
            pltpu.SemaphoreType.DMA((3,)),
            pltpu.SemaphoreType.DMA((SWEEPS + 1, 4)),
            pltpu.SemaphoreType.DMA((SWEEPS + 1, 4)),
        ],
        compiler_params=pltpu.CompilerParams(
            collective_id=0, has_side_effects=True, vmem_limit_bytes=60 * 2**20
        ),
    )(
        place.reshape(1, slots),
        depth.reshape(1, blocks),
        tile,
        side,
        turn,
        warmth,
        forcing,
        kappa,
    )


def solution(mesh):
    both = ("gx", "gy")
    devices = mesh.shape["gx"] * mesh.shape["gy"]
    return jax.shard_map(
        functools.partial(local, devices=devices, minor=mesh.shape["gy"]),
        mesh=mesh,
        in_specs=(
            P(both),
            P(both, None),
            P(both, None),
            P(both, None),
            P(both),
            P(None, both),
            P(None, both),
            P(None, both),
        ),
        out_specs=P(both, None),
        check_vma=False,
    )
```

```python
import functools

import jax
import jax.numpy as jnp
from jax import lax
from jax.experimental import pallas as pl
from jax.experimental.pallas import tpu as pltpu
from jax.sharding import PartitionSpec as P

B = 16
PLANE = B * B
CELLS = B * B * B
SWEEPS = 3
MASS_TERM = 4.0
LOWER_BOUND = 0.25
UPPER_BOUND = 2.0
CHUNK = 64
PARTS = 4
PLANES = B // PARTS
EARLY = 2
PAD = PLANE
LEVELS = 32767.0
F32 = jnp.float32
BF16 = jnp.bfloat16
I32 = jnp.int32
MESH = pl.DeviceIdType.MESH


def dot(a, b):
    return jnp.dot(a, b, preferred_element_type=F32)


def plane_rows(ref, base, face):
    if face == 0:
        return ref[pl.ds(base, PLANE), :]
    if face == 1:
        return ref[pl.ds(base + 15 * PLANE, PLANE), :]
    if face in (2, 3):
        first = base + (0 if face == 2 else PLANE - B)
        return jnp.concatenate([ref[pl.ds(first + PLANE * u, B), :] for u in range(B)], axis=0)
    return ref[pl.ds(base + (0 if face == 4 else B - 1), PLANE, stride=B), :]


def crossed_groups(ref, base, face):
    if face < 2:
        first, step, stride = base + 15 * PLANE * face, 1, B
    elif face < 4:
        first, step, stride = base + (PLANE - B) * (face - 2), 1, PLANE
    else:
        first, step, stride = base + (B - 1) * (face - 4), B, PLANE
    return [ref[pl.ds(first + step * v, B, stride=stride), :] for v in range(B)]


def face_update(ref, base, face, added):
    if face < 2:
        at = pl.ds(base + 15 * PLANE * face, PLANE)
        ref[at, :] = ref[at, :] + added
    elif face < 4:
        first = base + (PLANE - B) * (face - 2)
        for u in range(B):
            at = pl.ds(first + PLANE * u, B)
            ref[at, :] = ref[at, :] + added[u * B : (u + 1) * B]
    else:
        at = pl.ds(base + (B - 1) * (face - 4), PLANE, stride=B)
        ref[at, :] = ref[at, :] + added


def harmonic(p, q):
    return 2.0 * p * q / (p + q)


def kernel(
    devices,
    minor,
    place_ref,
    depth_ref,
    tile_ref,
    side_ref,
    turn_ref,
    warm_hbm,
    heat_hbm,
    kappa_hbm,
    out_ref,
    warm_in,
    heat_in,
    kappa_in,
    meta_out,
    meta_got,
    words_out,
    words_got,
    heat_out,
    heat_got,
    onehot,
    settle,
    conduct,
    link_i,
    link_j,
    link_k,
    right,
    inverse,
    field_a,
    field_b,
    change,
    gather,
    choose,
    turned,
    high,
    low,
    leaving,
    arriving,
    face_link,
    near,
    load_sem,
    meta_sems,
    send_sems,
    recv_sems,
    part_send,
    part_recv,
    face_send,
    face_recv,
):
    major = devices // minor
    gx = lax.axis_index("gx")
    gy = lax.axis_index("gy")
    me = gx * minor + gy
    slots = place_ref.shape[1]
    lanes = 128
    barrier = pltpu.get_barrier_semaphore()

    def peer(t):
        p = lax.rem(me + t * 37, devices)
        return p, (lax.div(p, minor), lax.rem(p, minor))

    def greet(t, carry):
        pl.semaphore_signal(barrier, inc=1, device_id=peer(t)[1], device_id_type=MESH)
        return carry

    loads = [
        pltpu.make_async_copy(kappa_hbm, kappa_in, load_sem.at[0]),
        pltpu.make_async_copy(warm_hbm, warm_in, load_sem.at[1]),
        pltpu.make_async_copy(heat_hbm, heat_in, load_sem.at[2]),
    ]
    for copy in loads:
        copy.start()
    lax.fori_loop(1, devices, greet, 0)

    place_row = place_ref[...].astype(F32)
    row_id = lax.broadcasted_iota(I32, (slots, slots), 0)
    col_id = lax.broadcasted_iota(I32, (slots, slots), 1)
    place_wide = jnp.broadcast_to(place_row, (slots, slots))
    place_col = jnp.sum(jnp.where(row_id == col_id, place_wide, 0.0), axis=1, keepdims=True)
    owner_row = jnp.floor(place_wide * (1.0 / lanes))
    owner_col = jnp.floor(place_col * (1.0 / lanes))
    again = jnp.sum(
        jnp.where((owner_row == owner_col) & (row_id < col_id), 1.0, 0.0), axis=0, keepdims=True
    )
    row_at = jnp.where(place_row >= 0.0, again * devices + owner_row[:1], -1.0)
    onehot[...] = jnp.where(row_id.astype(F32) == row_at, 1.0, 0.0).astype(BF16)
    tag_col = jnp.where(place_col >= 0.0, place_col - owner_col * lanes + 1.0, 0.0)
    tags = dot(onehot[...], jnp.broadcast_to(tag_col, (slots, lanes)).astype(BF16))

    def put_words(ref, field, t, planes, words):
        for s in range(2):
            ref[field, pl.ds(s * planes + t, devices, stride=2 * planes), :] = words[
                s * devices : (s + 1) * devices
            ]

    def send_words(out, got, field, rows, sem_out, sem_got):
        def block(p):
            return pl.ds(pl.multiple_of(p * rows, rows), rows)

        def one(t, carry):
            p, where = peer(t)
            pltpu.make_async_remote_copy(
                out.at[field, block(p)],
                got.at[field, block(me)],
                sem_out.at[field],
                sem_got.at[field],
                device_id=where,
                device_id_type=MESH,
            ).start()
            return carry

        lax.fori_loop(1, devices, one, 0)
        got[field, block(me), :] = out[field, block(me), :]

    def send_field(field):
        send_words(words_out, words_got, field, 2 * B, send_sems, recv_sems)

    def send_part(part):
        send_words(heat_out, heat_got, part, 2 * PLANES, part_send, part_recv)

    loads[0].wait()

    def pack_kappa(t, carry):
        both = dot(onehot[...], kappa_in[:, pl.ds(pl.multiple_of(t * PLANE, PLANE), PLANE)])
        ints = (both * 256.0).astype(I32)
        put_words(words_out, 0, t, B, ints[:, :lanes] + ints[:, lanes:] * 65536)
        return carry

    lax.fori_loop(0, B, pack_kappa, 0, unroll=2)
    pl.semaphore_wait(barrier, devices - 1)
    send_field(0)

    loads[1].wait()
    loads[2].wait()

    def scale_of(ref):
        def one(t, best):
            at = pl.ds(pl.multiple_of(t * lanes, lanes), lanes)
            return jnp.maximum(best, jnp.abs(ref[:, at].astype(F32)))

        best = lax.fori_loop(0, CELLS // lanes, one, jnp.zeros((slots, lanes), F32))
        largest = jnp.maximum(jnp.max(best, axis=1, keepdims=True) * 1.005, 1e-30)
        return dot(onehot[...], jnp.broadcast_to(largest, (slots, lanes)).astype(BF16))

    warm_scale = scale_of(warm_in)
    heat_scale = scale_of(heat_in)
    lane_id = lax.broadcasted_iota(I32, (devices, lanes), 1)
    meta = jnp.zeros((devices, lanes), F32)
    for n, part in enumerate((tags, warm_scale, heat_scale)):
        for s in range(2):
            meta = jnp.where(lane_id == 2 * n + s, part[s * devices : (s + 1) * devices], meta)
    meta_out[...] = meta.reshape(devices, 1, lanes)
    meta_got[pl.ds(me, 1)] = meta_out[pl.ds(me, 1)]

    def send_meta(t, carry):
        p, where = peer(t)
        pltpu.make_async_remote_copy(
            meta_out.at[p],
            meta_got.at[me],
            meta_sems.at[0],
            meta_sems.at[1],
            device_id=where,
            device_id_type=MESH,
        ).start()
        return carry

    lax.fori_loop(1, devices, send_meta, 0)

    def factor(scale):
        return jnp.where(scale > 0.0, LEVELS / jnp.maximum(scale, 1e-31), 0.0)

    warm_factor = factor(warm_scale)
    heat_factor = factor(heat_scale)

    def words_of(both, scale):
        ints = [jnp.round(both[:, c * lanes : (c + 1) * lanes] * scale).astype(I32) for c in (0, 1)]
        return ints[0] + ints[1] * 65536

    def pack_warm(t, carry):
        value = warm_in[:, pl.ds(pl.multiple_of(t * PLANE, PLANE), PLANE)]
        top = value.astype(BF16)
        rest = (value - top.astype(F32)).astype(BF16)
        both = dot(onehot[...], top) + dot(onehot[...], rest)
        put_words(words_out, 1, t, B, words_of(both, warm_factor))
        return carry

    lax.fori_loop(0, B, pack_warm, 0, unroll=2)
    send_field(1)

    def pack_heat(t, carry):
        both = dot(onehot[...], heat_in[:, pl.ds(pl.multiple_of(t * PLANE, PLANE), PLANE)])
        put_words(heat_out, t // PLANES, t % PLANES, PLANES, words_of(both, heat_factor))
        return carry

    lax.fori_loop(0, B, pack_heat, 0, unroll=2)
    for part in range(EARLY):
        send_part(part)

    swaps, flip_rows, flip_cols, linked = [], [], [], []
    ways = []
    sources = []
    for f in range(6):
        tile = tile_ref[f : f + 1, :]
        turn = turn_ref[f : f + 1, :]
        owner = tile >> 7
        inside = tile & 127
        live = tile >= 0
        way = jnp.where(
            owner == me - minor,
            0,
            jnp.where(owner == me + minor, 1, jnp.where(owner == me - 1, 2, 3)),
        )
        way = jnp.where(owner == me, -1, way)
        way = jnp.where(live, way, -2)
        ways.append(way)
        source = jnp.where(way == -1, side_ref[f : f + 1, :] * lanes + inside, 6 * lanes + way * lanes + inside)
        sources.append(jnp.where(live, source, -1))
        swap = turn >> 2
        bit_0 = turn & 1
        bit_1 = (turn >> 1) & 1
        swaps.append(jnp.broadcast_to(swap, (B, lanes)) > 0)
        flip_rows.append(jnp.broadcast_to(jnp.where(swap > 0, bit_1, bit_0), (B, lanes)) > 0)
        flip_cols.append(jnp.broadcast_to(jnp.where(swap > 0, bit_0, bit_1), (B, lanes)) > 0)
        linked.append(jnp.broadcast_to(tile, (PLANE, lanes)) >= 0)
    square = lax.broadcasted_iota(I32, (lanes, lanes), 0)
    across = lax.broadcasted_iota(I32, (lanes, lanes), 1)
    for f in range(6):
        at = pl.ds(f * lanes, lanes)
        for n in range(10):
            gather[pl.ds(n * lanes, lanes), at] = jnp.where(
                square + n * lanes == sources[f], 1.0, 0.0
            ).astype(BF16)
        for d in range(4):
            choose[at, pl.ds(d * lanes, lanes)] = jnp.where(
                (square == across) & (ways[f] == d), 1.0, 0.0
            ).astype(BF16)
    for ref in (conduct, link_i, link_j, link_k, field_a, field_b):
        fill = jnp.full((PAD, lanes), 1.0 if ref is conduct else 0.0, F32)
        ref[pl.ds(0, PAD), :] = fill
        ref[pl.ds(PAD + CELLS, PAD), :] = fill

    neighbours = (
        (lax.rem(gx + major - 1, major), gy),
        (lax.rem(gx + 1, major), gy),
        (gx, lax.rem(gy + minor - 1, minor)),
        (gx, lax.rem(gy + 1, minor)),
    )

    def face_copies(round_):
        return [
            pltpu.make_async_remote_copy(
                leaving.at[round_, d],
                arriving.at[round_, d ^ 1],
                face_send.at[round_, d],
                face_recv.at[round_, d ^ 1],
                device_id=neighbours[d],
                device_id_type=MESH,
            )
            for d in range(4)
        ]

    def start_faces(ref, round_):
        for f in range(6):
            plain = plane_rows(ref, PAD, f)
            crossed = crossed_groups(ref, PAD, f)
            laid = [
                jnp.where(swaps[f], plain[c * B : (c + 1) * B], crossed[c]) for c in range(B)
            ]
            for c in range(B):
                turned[pl.ds(f * PLANE + c * B, B), :] = jnp.where(
                    flip_cols[f], laid[B - 1 - c], laid[c]
                )
        for f in range(6):
            back = [turned[pl.ds(f * PLANE + r, B, stride=B), :] for r in range(B)]
            plane = jnp.concatenate(
                [jnp.where(flip_rows[f], back[B - 1 - r], back[r]) for r in range(B)], axis=0
            )
            top = plane.astype(BF16)
            at = pl.ds(f * lanes, lanes)
            high[min(round_, 1), :, at] = top
            if round_ > 0:
                low[:, at] = (plane - top.astype(F32)).astype(BF16)
        for d in range(4):
            leaving[round_, d] = dot(high[min(round_, 1)], choose[:, pl.ds(d * lanes, lanes)]).astype(BF16)
        for copy in face_copies(round_):
            copy.start()

    def finish_faces(round_, use):
        for pair in range(3):
            at = pl.ds(pair * 2 * lanes, 2 * lanes)
            planes = dot(high[min(round_, 1)], gather[pl.ds(0, 6 * lanes), at])
            if round_ > 0:
                planes = planes + dot(low[...], gather[pl.ds(0, 6 * lanes), at])
            near[:, at] = planes
        for copy in face_copies(round_):
            copy.wait_recv()
        far = jnp.concatenate([arriving[round_, d] for d in range(4)], axis=1)
        for pair in range(3):
            at = pl.ds(pair * 2 * lanes, 2 * lanes)
            planes = near[:, at] + dot(far, gather[pl.ds(6 * lanes, 4 * lanes), at])
            use(2 * pair, planes[:, :lanes])
            use(2 * pair + 1, planes[:, lanes:])

    def arrived(sems, sem, buffer):
        pltpu.make_async_copy(buffer, buffer, sems.at[sem]).wait()

    def all_but_mine(field):
        return words_got.at[field, pl.ds(0, (devices - 1) * 2 * B)]

    arrived(meta_sems, 1, meta_got.at[pl.ds(0, devices - 1)])
    meta = meta_got[...].reshape(devices, lanes)
    spread = [
        jnp.concatenate(
            [jnp.broadcast_to(meta[:, 2 * n + s : 2 * n + s + 1], (devices, lanes)) for s in range(2)],
            axis=0,
        )
        for n in range(3)
    ]
    block_id = lax.broadcasted_iota(I32, (2 * devices, lanes), 1).astype(F32)
    chosen = jnp.where(spread[0] == block_id + 1.0, 1.0, 0.0)
    warm_unit = jnp.sum(chosen * spread[1], axis=0, keepdims=True) * (1.0 / LEVELS)
    heat_scale_row = jnp.sum(chosen * spread[2], axis=0, keepdims=True) * (MASS_TERM / LEVELS)
    by_block = chosen.T
    settle[:, : 2 * devices] = (by_block * 256.0).astype(BF16)
    settle[:, 2 * devices :] = by_block.astype(BF16)

    def words_at(ref, field, t, planes):
        words = jnp.concatenate(
            [ref[field, pl.ds(s * planes + t, devices, stride=2 * planes), :] for s in range(2)], axis=0
        )
        second = (words + 32768) >> 16
        first = words - second * 65536
        return jnp.concatenate([first, second], axis=1)

    def placed_16(ref, field, t, planes):
        ints = words_at(ref, field, t, planes)
        top = ints >> 8
        rest = ints & 255
        parts = jnp.concatenate([top.astype(F32).astype(BF16), rest.astype(F32).astype(BF16)], axis=0)
        return dot(settle[...], parts).T

    depth = depth_ref[...]
    level = jnp.where(depth == 0, 1.0, jnp.where(depth == 1, 4.0, 16.0)) * (1.0 / 256.0)

    def rows_of(t):
        return pl.ds(pl.multiple_of(PAD + t * PLANE, PLANE), PLANE)

    arrived(recv_sems, 0, all_but_mine(0))

    def place_kappa(t, carry):
        ints = words_at(words_got, 0, t, B).astype(F32).astype(BF16)
        conduct[rows_of(t), :] = dot(settle[:, 2 * devices :], ints).T * level
        return carry

    lax.fori_loop(0, B, place_kappa, 0, unroll=2)
    start_faces(conduct, 0)
    for part in range(EARLY, PARTS):
        send_part(part)

    row_in = lax.broadcasted_iota(I32, (CHUNK, lanes), 0)
    inner_k = (row_in & (B - 1)) < B - 1
    chunks = CELLS // CHUNK

    def at_chunk(n, shift=0):
        return pl.ds(pl.multiple_of(PAD + n * CHUNK, CHUNK) + shift, CHUNK)

    def make_links(n, carry):
        here = conduct[at_chunk(n), :]
        row = row_in + n * CHUNK
        link_i[at_chunk(n), :] = jnp.where(
            row < CELLS - PLANE, harmonic(here, conduct[at_chunk(n, PLANE), :]), 0.0
        )
        link_j[at_chunk(n), :] = jnp.where(
            (row & (PLANE - 1)) < PLANE - B, harmonic(here, conduct[at_chunk(n, B), :]), 0.0
        )
        link_k[at_chunk(n), :] = jnp.where(inner_k, harmonic(here, conduct[at_chunk(n, 1), :]), 0.0)
        return carry

    lax.fori_loop(0, chunks, make_links, 0, unroll=2)

    def add_links(n, carry):
        inverse[at_chunk(n), :] = (
            MASS_TERM
            + link_i[at_chunk(n), :]
            + link_i[at_chunk(n, -PLANE), :]
            + link_j[at_chunk(n), :]
            + link_j[at_chunk(n, -B), :]
            + link_k[at_chunk(n), :]
            + link_k[at_chunk(n, -1), :]
        )
        return carry

    lax.fori_loop(0, chunks, add_links, 0, unroll=2)

    arrived(recv_sems, 1, all_but_mine(1))

    def place_warm(t, carry):
        field_a[rows_of(t), :] = placed_16(words_got, 1, t, B) * warm_unit
        return carry

    lax.fori_loop(0, B, place_warm, 0, unroll=2)
    start_faces(field_a, 1)

    def inner_sum(now, n):
        return (
            link_i[at_chunk(n), :] * now[at_chunk(n, PLANE), :]
            + link_i[at_chunk(n, -PLANE), :] * now[at_chunk(n, -PLANE), :]
            + link_j[at_chunk(n), :] * now[at_chunk(n, B), :]
            + link_j[at_chunk(n, -B), :] * now[at_chunk(n, -B), :]
            + link_k[at_chunk(n), :] * now[at_chunk(n, 1), :]
            + link_k[at_chunk(n, -1), :] * now[at_chunk(n, -1), :]
        )

    def first_sum(n, carry):
        change[at_chunk(n), :] = MASS_TERM * field_a[at_chunk(n), :] + inner_sum(field_a, n)
        return carry

    lax.fori_loop(0, chunks, first_sum, 0, unroll=2)

    def make_face_links(f, planes):
        links = jnp.where(
            linked[f], harmonic(plane_rows(conduct, PAD, f), jnp.where(linked[f], planes, 1.0)), 0.0
        )
        face_link[f] = links
        face_update(inverse, PAD, f, links)

    finish_faces(0, make_face_links)

    def invert(n, carry):
        inverse[at_chunk(n), :] = 1.0 / inverse[at_chunk(n), :]
        return carry

    lax.fori_loop(0, chunks, invert, 0, unroll=2)

    def first_faces(f, planes):
        face_update(change, PAD, f, face_link[f] * planes)
        face_link[f] = face_link[f] * plane_rows(inverse, PAD, f)

    finish_faces(1, first_faces)

    centre = 0.5 * (UPPER_BOUND + LOWER_BOUND)
    half_width = 0.5 * (UPPER_BOUND - LOWER_BOUND)
    relative = centre / half_width
    ratio = 1.0 / relative

    for part in range(PARTS):
        arrived(part_recv, part, heat_got.at[part, pl.ds(0, (devices - 1) * 2 * PLANES)])

        def place_heat(t, carry, part=part):
            at = rows_of(t + part * PLANES)
            here = field_a[at, :]
            added = placed_16(heat_got, part, t, PLANES) * heat_scale_row
            right[at, :] = MASS_TERM * here + added
            step = (1.0 / centre) * ((change[at, :] + added) * inverse[at, :] - here)
            change[at, :] = step
            field_b[at, :] = here + step
            return carry

        lax.fori_loop(0, PLANES, place_heat, 0, unroll=2)

    now, then = field_b, field_a
    for sweep in range(1, SWEEPS):
        ratio_next = 1.0 / (2.0 * relative - ratio)
        keep, gain = ratio_next * ratio, 2.0 * ratio_next / half_width
        ratio = ratio_next
        start_faces(now, sweep + 1)

        def relax(n, carry, now=now, then=then, keep=keep, gain=gain, sweep=sweep):
            here = now[at_chunk(n), :]
            pulled = right[at_chunk(n), :] + inner_sum(now, n)
            step = gain * (pulled * inverse[at_chunk(n), :] - here) + keep * change[at_chunk(n), :]
            if sweep < SWEEPS - 1:
                change[at_chunk(n), :] = step
            then[at_chunk(n), :] = here + step
            return carry

        lax.fori_loop(0, chunks, relax, 0, unroll=2)

        def add_faces(f, planes, then=then, gain=gain, sweep=sweep):
            added = gain * face_link[f] * planes
            face_update(then, PAD, f, added)
            if sweep < SWEEPS - 1:
                face_update(change, PAD, f, added)

        finish_faces(sweep + 1, add_faces)
        now, then = then, now

    def write_out(t, carry):
        out_ref[:, pl.ds(pl.multiple_of(t * PLANE, PLANE), PLANE)] = now[rows_of(t), :].T
        return carry

    lax.fori_loop(0, B, write_out, 0, unroll=2)

    for round_ in range(SWEEPS + 1):
        for copy in face_copies(round_):
            copy.wait_send()
    arrived(meta_sems, 0, meta_out.at[pl.ds(0, devices - 1)])
    for field in range(2):
        arrived(send_sems, field, words_out.at[field, pl.ds(0, (devices - 1) * 2 * B)])
    for part in range(PARTS):
        arrived(part_send, part, heat_out.at[part, pl.ds(0, (devices - 1) * 2 * PLANES)])


def local(place, warmth, forcing, kappa, depth, tile, side, turn, devices, minor):
    slots = place.shape[0]
    blocks = depth.shape[0]
    lanes = 128
    tall = CELLS + 2 * PAD
    vmem = pl.BlockSpec(memory_space=pltpu.VMEM)
    hbm = pl.BlockSpec(memory_space=pl.ANY)
    tall_field = pltpu.VMEM((tall, lanes), F32)
    return pl.pallas_call(
        functools.partial(kernel, devices, minor),
        out_shape=pltpu.VMEM((blocks, CELLS), F32),
        in_specs=[vmem] * 5 + [hbm] * 3,
        out_specs=vmem,
        scratch_shapes=[
            pltpu.VMEM((slots, CELLS), F32),
            pltpu.VMEM((slots, CELLS), BF16),
            pltpu.VMEM((slots, CELLS), BF16),
            pltpu.VMEM((devices, 1, lanes), F32),
            pltpu.VMEM((devices, 1, lanes), F32),
            pltpu.VMEM((2, devices * 2 * B, lanes), I32),
            pltpu.VMEM((2, devices * 2 * B, lanes), I32),
            pltpu.VMEM((PARTS, devices * 2 * PLANES, lanes), I32),
            pltpu.VMEM((PARTS, devices * 2 * PLANES, lanes), I32),
            pltpu.VMEM((slots, slots), BF16),
            pltpu.VMEM((blocks, 4 * devices), BF16),
            tall_field,
            tall_field,
            tall_field,
            tall_field,
            tall_field,
            tall_field,
            tall_field,
            tall_field,
            tall_field,
            pltpu.VMEM((10 * lanes, 6 * lanes), BF16),
            pltpu.VMEM((6 * lanes, 4 * lanes), BF16),
            pltpu.VMEM((6 * PLANE, lanes), F32),
            pltpu.VMEM((2, PLANE, 6 * lanes), BF16),
            pltpu.VMEM((PLANE, 6 * lanes), BF16),
            pltpu.VMEM((SWEEPS + 1, 4, PLANE, lanes), BF16),
            pltpu.VMEM((SWEEPS + 1, 4, PLANE, lanes), BF16),
            pltpu.VMEM((6, PLANE, lanes), F32),
            pltpu.VMEM((PLANE, 6 * lanes), F32),
            pltpu.SemaphoreType.DMA((3,)),
            pltpu.SemaphoreType.DMA((2,)),
            pltpu.SemaphoreType.DMA((2,)),
            pltpu.SemaphoreType.DMA((2,)),
            pltpu.SemaphoreType.DMA((PARTS,)),
            pltpu.SemaphoreType.DMA((PARTS,)),
            pltpu.SemaphoreType.DMA((SWEEPS + 1, 4)),
            pltpu.SemaphoreType.DMA((SWEEPS + 1, 4)),
        ],
        compiler_params=pltpu.CompilerParams(
            collective_id=0, has_side_effects=True, vmem_limit_bytes=54 * 2**20
        ),
    )(
        place.reshape(1, slots),
        depth.reshape(1, blocks),
        tile,
        side,
        turn,
        warmth,
        forcing,
        kappa,
    )


def solution(mesh):
    both = ("gx", "gy")
    devices = mesh.shape["gx"] * mesh.shape["gy"]
    return jax.shard_map(
        functools.partial(local, devices=devices, minor=mesh.shape["gy"]),
        mesh=mesh,
        in_specs=(
            P(both),
            P(both, None),
            P(both, None),
            P(both, None),
            P(both),
            P(None, both),
            P(None, both),
            P(None, both),
        ),
        out_specs=P(both, None),
        check_vma=False,
    )
```

```python
import functools

import jax
import jax.numpy as jnp
from jax import lax
from jax.experimental import pallas as pl
from jax.experimental.pallas import tpu as pltpu
from jax.sharding import PartitionSpec as P

B = 16
PLANE = B * B
CELLS = B * B * B
SWEEPS = 3
MASS_TERM = 4.0
LOWER_BOUND = 0.25
UPPER_BOUND = 2.0
CHUNK = 64
PARTS = 4
FACE_CAP = 32
PLANES = B // PARTS
EARLY = 2
LATE = 3
PAD = PLANE
LEVELS = 32767.0
F32 = jnp.float32
BF16 = jnp.bfloat16
I32 = jnp.int32
MESH = pl.DeviceIdType.MESH


def dot(a, b):
    return jnp.dot(a, b, preferred_element_type=F32)


def plane_rows(ref, base, face):
    if face == 0:
        return ref[pl.ds(base, PLANE), :]
    if face == 1:
        return ref[pl.ds(base + 15 * PLANE, PLANE), :]
    if face in (2, 3):
        first = base + (0 if face == 2 else PLANE - B)
        return jnp.concatenate([ref[pl.ds(first + PLANE * u, B), :] for u in range(B)], axis=0)
    return ref[pl.ds(base + (0 if face == 4 else B - 1), PLANE, stride=B), :]


def crossed_groups(ref, base, face):
    if face < 2:
        first, step, stride = base + 15 * PLANE * face, 1, B
    elif face < 4:
        first, step, stride = base + (PLANE - B) * (face - 2), 1, PLANE
    else:
        first, step, stride = base + (B - 1) * (face - 4), B, PLANE
    return [ref[pl.ds(first + step * v, B, stride=stride), :] for v in range(B)]


def face_update(ref, base, face, added):
    if face < 2:
        at = pl.ds(base + 15 * PLANE * face, PLANE)
        ref[at, :] = ref[at, :] + added
    elif face < 4:
        first = base + (PLANE - B) * (face - 2)
        for u in range(B):
            at = pl.ds(first + PLANE * u, B)
            ref[at, :] = ref[at, :] + added[u * B : (u + 1) * B]
    else:
        at = pl.ds(base + (B - 1) * (face - 4), PLANE, stride=B)
        ref[at, :] = ref[at, :] + added


def harmonic(p, q):
    return 2.0 * p * q / (p + q)


def kernel(
    devices,
    minor,
    place_ref,
    depth_ref,
    tile_ref,
    side_ref,
    turn_ref,
    warm_hbm,
    heat_hbm,
    kappa_hbm,
    out_ref,
    warm_in,
    heat_in,
    kappa_in,
    meta_out,
    meta_got,
    words_out,
    words_got,
    heat_out,
    heat_got,
    onehot,
    settle,
    conduct,
    link_i,
    link_j,
    link_k,
    right,
    inverse,
    field_a,
    field_b,
    change,
    gather,
    choose,
    turned,
    picked,
    high,
    low,
    leaving,
    arriving,
    face_link,
    near,
    load_sem,
    meta_sems,
    send_sems,
    recv_sems,
    part_send,
    part_recv,
    face_send,
    face_recv,
):
    major = devices // minor
    gx = lax.axis_index("gx")
    gy = lax.axis_index("gy")
    me = gx * minor + gy
    slots = place_ref.shape[1]
    lanes = 128
    barrier = pltpu.get_barrier_semaphore()

    def peer(t):
        p = lax.rem(me + t * 37, devices)
        return p, (lax.div(p, minor), lax.rem(p, minor))

    def greet(t, carry):
        pl.semaphore_signal(barrier, inc=1, device_id=peer(t)[1], device_id_type=MESH)
        return carry

    loads = [
        pltpu.make_async_copy(kappa_hbm, kappa_in, load_sem.at[0]),
        pltpu.make_async_copy(warm_hbm, warm_in, load_sem.at[1]),
        pltpu.make_async_copy(heat_hbm, heat_in, load_sem.at[2]),
    ]
    for copy in loads:
        copy.start()
    lax.fori_loop(1, devices, greet, 0)

    place_row = place_ref[...].astype(F32)
    row_id = lax.broadcasted_iota(I32, (slots, slots), 0)
    col_id = lax.broadcasted_iota(I32, (slots, slots), 1)
    place_wide = jnp.broadcast_to(place_row, (slots, slots))
    place_col = jnp.sum(jnp.where(row_id == col_id, place_wide, 0.0), axis=1, keepdims=True)
    owner_row = jnp.floor(place_wide * (1.0 / lanes))
    owner_col = jnp.floor(place_col * (1.0 / lanes))
    again = jnp.sum(
        jnp.where((owner_row == owner_col) & (row_id < col_id), 1.0, 0.0), axis=0, keepdims=True
    )
    row_at = jnp.where(place_row >= 0.0, again * devices + owner_row[:1], -1.0)
    onehot[...] = jnp.where(row_id.astype(F32) == row_at, 1.0, 0.0).astype(BF16)
    tag_col = jnp.where(place_col >= 0.0, place_col - owner_col * lanes + 1.0, 0.0)
    tags = dot(onehot[...], jnp.broadcast_to(tag_col, (slots, lanes)).astype(BF16))

    def put_words(ref, field, t, planes, words):
        for s in range(2):
            ref[field, pl.ds(s * planes + t, devices, stride=2 * planes), :] = words[
                s * devices : (s + 1) * devices
            ]

    def send_words(out, got, field, rows, sem_out, sem_got):
        def block(p):
            return pl.ds(pl.multiple_of(p * rows, rows), rows)

        def one(t, carry):
            p, where = peer(t)
            pltpu.make_async_remote_copy(
                out.at[field, block(p)],
                got.at[field, block(me)],
                sem_out.at[field],
                sem_got.at[field],
                device_id=where,
                device_id_type=MESH,
            ).start()
            return carry

        lax.fori_loop(1, devices, one, 0)
        got[field, block(me), :] = out[field, block(me), :]

    def send_field(field):
        send_words(words_out, words_got, field, 2 * B, send_sems, recv_sems)

    def send_part(part):
        send_words(heat_out, heat_got, part, 2 * PLANES, part_send, part_recv)

    loads[0].wait()

    def pack_kappa(t, carry):
        both = dot(onehot[...], kappa_in[:, pl.ds(pl.multiple_of(t * PLANE, PLANE), PLANE)])
        ints = (both * 256.0).astype(I32)
        put_words(words_out, 0, t, B, ints[:, :lanes] + ints[:, lanes:] * 65536)
        return carry

    lax.fori_loop(0, B, pack_kappa, 0, unroll=2)
    pl.semaphore_wait(barrier, devices - 1)
    send_field(0)

    loads[1].wait()
    loads[2].wait()

    def scale_of(ref):
        def one(t, best):
            at = pl.ds(pl.multiple_of(t * lanes, lanes), lanes)
            return jnp.maximum(best, jnp.abs(ref[:, at].astype(F32)))

        best = lax.fori_loop(0, CELLS // lanes, one, jnp.zeros((slots, lanes), F32))
        largest = jnp.maximum(jnp.max(best, axis=1, keepdims=True) * 1.005, 1e-30)
        return dot(onehot[...], jnp.broadcast_to(largest, (slots, lanes)).astype(BF16))

    warm_scale = scale_of(warm_in)
    heat_scale = scale_of(heat_in)
    lane_id = lax.broadcasted_iota(I32, (devices, lanes), 1)
    meta = jnp.zeros((devices, lanes), F32)
    for n, part in enumerate((tags, warm_scale, heat_scale)):
        for s in range(2):
            meta = jnp.where(lane_id == 2 * n + s, part[s * devices : (s + 1) * devices], meta)
    meta_out[...] = meta.reshape(devices, 1, lanes)
    meta_got[pl.ds(me, 1)] = meta_out[pl.ds(me, 1)]

    def send_meta(t, carry):
        p, where = peer(t)
        pltpu.make_async_remote_copy(
            meta_out.at[p],
            meta_got.at[me],
            meta_sems.at[0],
            meta_sems.at[1],
            device_id=where,
            device_id_type=MESH,
        ).start()
        return carry

    lax.fori_loop(1, devices, send_meta, 0)

    def factor(scale):
        return jnp.where(scale > 0.0, LEVELS / jnp.maximum(scale, 1e-31), 0.0)

    warm_factor = factor(warm_scale)
    heat_factor = factor(heat_scale)

    def words_of(both, scale):
        ints = [jnp.round(both[:, c * lanes : (c + 1) * lanes] * scale).astype(I32) for c in (0, 1)]
        return ints[0] + ints[1] * 65536

    def pack_warm(t, carry):
        value = warm_in[:, pl.ds(pl.multiple_of(t * PLANE, PLANE), PLANE)]
        top = value.astype(BF16)
        rest = (value - top.astype(F32)).astype(BF16)
        both = dot(onehot[...], top) + dot(onehot[...], rest)
        put_words(words_out, 1, t, B, words_of(both, warm_factor))
        return carry

    lax.fori_loop(0, B, pack_warm, 0, unroll=2)
    send_field(1)

    def pack_heat(t, carry):
        both = dot(onehot[...], heat_in[:, pl.ds(pl.multiple_of(t * PLANE, PLANE), PLANE)])
        put_words(heat_out, t // PLANES, t % PLANES, PLANES, words_of(both, heat_factor))
        return carry

    lax.fori_loop(0, B, pack_heat, 0, unroll=2)
    for part in range(EARLY):
        send_part(part)

    swaps, flip_rows, flip_cols, linked = [], [], [], []
    ways = []
    insides = []
    turn_bits = []
    for f in range(6):
        tile = tile_ref[f : f + 1, :]
        turn = turn_ref[f : f + 1, :]
        owner = tile >> 7
        inside = tile & 127
        live = tile >= 0
        way = jnp.where(
            owner == me - minor,
            0,
            jnp.where(owner == me + minor, 1, jnp.where(owner == me - 1, 2, 3)),
        )
        way = jnp.where(owner == me, -1, way)
        way = jnp.where(live, way, -2)
        ways.append(way)
        insides.append(inside)
        swap = turn >> 2
        bit_0 = turn & 1
        bit_1 = (turn >> 1) & 1
        turn_bits.append(
            [swap, jnp.where(swap > 0, bit_1, bit_0), jnp.where(swap > 0, bit_0, bit_1)]
        )
        swaps.append(jnp.broadcast_to(swap, (B, lanes)) > 0)
        flip_rows.append(jnp.broadcast_to(jnp.where(swap > 0, bit_1, bit_0), (B, lanes)) > 0)
        flip_cols.append(jnp.broadcast_to(jnp.where(swap > 0, bit_0, bit_1), (B, lanes)) > 0)
        linked.append(jnp.broadcast_to(tile, (PLANE, lanes)) >= 0)
    square = lax.broadcasted_iota(I32, (lanes, lanes), 0)
    across = lax.broadcasted_iota(I32, (lanes, lanes), 1)
    def column(row):
        return jnp.sum(jnp.where(square == across, row, 0.0), axis=1, keepdims=True)

    def below(counts, limit):
        return jnp.sum(jnp.where(square < limit, counts, 0.0), axis=0, keepdims=True)

    ranks, theirs = [], []
    for d in range(4):
        sends = sum(jnp.where(ways[f] == d, 1.0, 0.0) for f in range(6))
        ranks.append(below(column(sends), across))
        marks = sum(
            jnp.where((square == insides[f]) & (ways[f] == d), 1.0, 0.0) for f in range(6)
        )
        theirs.append(jnp.sum(marks, axis=1, keepdims=True))
    for f in range(6):
        at = pl.ds(f * lanes, lanes)
        source = jnp.where(
            ways[f] == -1, (side_ref[f : f + 1, :] * lanes + insides[f]).astype(F32), -1.0
        )
        lane = jnp.full((1, lanes), -1.0, F32)
        for d in range(4):
            slot = below(theirs[d], insides[f])
            source = jnp.where(ways[f] == d, (6 + d) * lanes + (d ^ 1) * FACE_CAP + slot, source)
            lane = jnp.where(ways[f] == d, d * FACE_CAP + ranks[d], lane)
        source = source.astype(I32)
        for n in range(10):
            gather[pl.ds(n * lanes, lanes), at] = jnp.where(
                square + n * lanes == source, 1.0, 0.0
            ).astype(BF16)
        choose[at, :] = jnp.where(column(lane) == across.astype(F32), 1.0, 0.0).astype(BF16)
    sent_bits = [
        jnp.broadcast_to(
            dot(
                jnp.concatenate(
                    [jnp.broadcast_to(turn_bits[f][n], (B, lanes)) for f in range(6)], axis=1
                ).astype(F32).astype(BF16),
                choose[...],
            ),
            (B, lanes),
        )
        > 0.5
        for n in range(3)
    ]
    for ref in (conduct, link_i, link_j, link_k, field_a, field_b):
        fill = jnp.full((PAD, lanes), 1.0 if ref is conduct else 0.0, F32)
        ref[pl.ds(0, PAD), :] = fill
        ref[pl.ds(PAD + CELLS, PAD), :] = fill

    neighbours = (
        (lax.rem(gx + major - 1, major), gy),
        (lax.rem(gx + 1, major), gy),
        (gx, lax.rem(gy + minor - 1, minor)),
        (gx, lax.rem(gy + 1, minor)),
    )

    def face_copies(round_):
        return [
            pltpu.make_async_remote_copy(
                leaving.at[round_],
                arriving.at[round_, d ^ 1],
                face_send.at[round_, d],
                face_recv.at[round_, d ^ 1],
                device_id=neighbours[d],
                device_id_type=MESH,
            )
            for d in range(4)
        ]

    def turn_planes(plain, crossed, scratch, swap, flip_col):
        laid = [jnp.where(swap, plain[c * B : (c + 1) * B], crossed[c]) for c in range(B)]
        for c in range(B):
            scratch[pl.ds(c * B, B), :] = jnp.where(flip_col, laid[B - 1 - c], laid[c])

    def turned_back(scratch, flip_row):
        back = [scratch[pl.ds(r, B, stride=B), :] for r in range(B)]
        return jnp.concatenate(
            [jnp.where(flip_row, back[B - 1 - r], back[r]) for r in range(B)], axis=0
        )

    def start_faces(ref, round_):
        which = min(round_, 1)
        for f in range(6):
            low[:, pl.ds(f * lanes, lanes)] = plane_rows(ref, PAD, f).astype(BF16)
        sent = dot(low[...], choose[...])
        picked[...] = sent
        crossed = [picked[pl.ds(v, B, stride=B), :] for v in range(B)]
        turn_planes(sent, crossed, turned.at[0], sent_bits[0], sent_bits[2])
        leaving[round_] = turned_back(turned.at[0], sent_bits[1]).astype(BF16)
        for copy in face_copies(round_):
            copy.start()
        for f in range(6):
            turn_planes(
                plane_rows(ref, PAD, f),
                crossed_groups(ref, PAD, f),
                turned.at[f],
                swaps[f],
                flip_cols[f],
            )
        for f in range(6):
            plane = turned_back(turned.at[f], flip_rows[f])
            top = plane.astype(BF16)
            at = pl.ds(f * lanes, lanes)
            high[which, :, at] = top
            if round_ > 0:
                low[:, at] = (plane - top.astype(F32)).astype(BF16)

    def finish_faces(round_, use):
        for pair in range(3):
            at = pl.ds(pair * 2 * lanes, 2 * lanes)
            planes = dot(high[min(round_, 1)], gather[pl.ds(0, 6 * lanes), at])
            if round_ > 0:
                planes = planes + dot(low[...], gather[pl.ds(0, 6 * lanes), at])
            near[:, at] = planes
        for copy in face_copies(round_):
            copy.wait_recv()
        far = jnp.concatenate([arriving[round_, d] for d in range(4)], axis=1)
        for pair in range(3):
            at = pl.ds(pair * 2 * lanes, 2 * lanes)
            planes = near[:, at] + dot(far, gather[pl.ds(6 * lanes, 4 * lanes), at])
            use(2 * pair, planes[:, :lanes])
            use(2 * pair + 1, planes[:, lanes:])

    def arrived(sems, sem, buffer):
        pltpu.make_async_copy(buffer, buffer, sems.at[sem]).wait()

    def all_but_mine(field):
        return words_got.at[field, pl.ds(0, (devices - 1) * 2 * B)]

    arrived(meta_sems, 1, meta_got.at[pl.ds(0, devices - 1)])
    meta = meta_got[...].reshape(devices, lanes)
    spread = [
        jnp.concatenate(
            [jnp.broadcast_to(meta[:, 2 * n + s : 2 * n + s + 1], (devices, lanes)) for s in range(2)],
            axis=0,
        )
        for n in range(3)
    ]
    block_id = lax.broadcasted_iota(I32, (2 * devices, lanes), 1).astype(F32)
    chosen = jnp.where(spread[0] == block_id + 1.0, 1.0, 0.0)
    warm_unit = jnp.sum(chosen * spread[1], axis=0, keepdims=True) * (1.0 / LEVELS)
    heat_scale_row = jnp.sum(chosen * spread[2], axis=0, keepdims=True) * (MASS_TERM / LEVELS)
    by_block = chosen.T
    settle[:, : 2 * devices] = (by_block * 256.0).astype(BF16)
    settle[:, 2 * devices :] = by_block.astype(BF16)

    def words_at(ref, field, t, planes):
        words = jnp.concatenate(
            [ref[field, pl.ds(s * planes + t, devices, stride=2 * planes), :] for s in range(2)], axis=0
        )
        second = (words + 32768) >> 16
        first = words - second * 65536
        return jnp.concatenate([first, second], axis=1)

    def placed_16(ref, field, t, planes):
        ints = words_at(ref, field, t, planes)
        top = ints >> 8
        rest = ints & 255
        parts = jnp.concatenate([top.astype(F32).astype(BF16), rest.astype(F32).astype(BF16)], axis=0)
        return dot(settle[...], parts).T

    depth = depth_ref[...]
    level = jnp.where(depth == 0, 1.0, jnp.where(depth == 1, 4.0, 16.0)) * (1.0 / 256.0)

    def rows_of(t):
        return pl.ds(pl.multiple_of(PAD + t * PLANE, PLANE), PLANE)

    arrived(recv_sems, 0, all_but_mine(0))

    def place_kappa(t, carry):
        ints = words_at(words_got, 0, t, B).astype(F32).astype(BF16)
        conduct[rows_of(t), :] = dot(settle[:, 2 * devices :], ints).T * level
        return carry

    lax.fori_loop(0, B, place_kappa, 0, unroll=2)
    start_faces(conduct, 0)
    for part in range(EARLY, LATE):
        send_part(part)

    row_in = lax.broadcasted_iota(I32, (CHUNK, lanes), 0)
    inner_k = (row_in & (B - 1)) < B - 1
    chunks = CELLS // CHUNK

    def at_chunk(n, shift=0):
        return pl.ds(pl.multiple_of(PAD + n * CHUNK, CHUNK) + shift, CHUNK)

    def make_links(n, carry):
        here = conduct[at_chunk(n), :]
        row = row_in + n * CHUNK
        link_i[at_chunk(n), :] = jnp.where(
            row < CELLS - PLANE, harmonic(here, conduct[at_chunk(n, PLANE), :]), 0.0
        )
        link_j[at_chunk(n), :] = jnp.where(
            (row & (PLANE - 1)) < PLANE - B, harmonic(here, conduct[at_chunk(n, B), :]), 0.0
        )
        link_k[at_chunk(n), :] = jnp.where(inner_k, harmonic(here, conduct[at_chunk(n, 1), :]), 0.0)
        return carry

    lax.fori_loop(0, chunks, make_links, 0, unroll=2)

    def add_links(n, carry):
        inverse[at_chunk(n), :] = (
            MASS_TERM
            + link_i[at_chunk(n), :]
            + link_i[at_chunk(n, -PLANE), :]
            + link_j[at_chunk(n), :]
            + link_j[at_chunk(n, -B), :]
            + link_k[at_chunk(n), :]
            + link_k[at_chunk(n, -1), :]
        )
        return carry

    lax.fori_loop(0, chunks, add_links, 0, unroll=2)

    arrived(recv_sems, 1, all_but_mine(1))

    def place_warm(t, carry):
        field_a[rows_of(t), :] = placed_16(words_got, 1, t, B) * warm_unit
        return carry

    lax.fori_loop(0, B, place_warm, 0, unroll=2)
    start_faces(field_a, 1)
    for part in range(LATE, PARTS):
        send_part(part)

    def inner_sum(now, n):
        return (
            link_i[at_chunk(n), :] * now[at_chunk(n, PLANE), :]
            + link_i[at_chunk(n, -PLANE), :] * now[at_chunk(n, -PLANE), :]
            + link_j[at_chunk(n), :] * now[at_chunk(n, B), :]
            + link_j[at_chunk(n, -B), :] * now[at_chunk(n, -B), :]
            + link_k[at_chunk(n), :] * now[at_chunk(n, 1), :]
            + link_k[at_chunk(n, -1), :] * now[at_chunk(n, -1), :]
        )

    def first_sum(n, carry):
        change[at_chunk(n), :] = MASS_TERM * field_a[at_chunk(n), :] + inner_sum(field_a, n)
        return carry

    lax.fori_loop(0, chunks, first_sum, 0, unroll=2)

    def make_face_links(f, planes):
        links = jnp.where(
            linked[f], harmonic(plane_rows(conduct, PAD, f), jnp.where(linked[f], planes, 1.0)), 0.0
        )
        face_link[f] = links
        face_update(inverse, PAD, f, links)

    finish_faces(0, make_face_links)

    def invert(n, carry):
        inverse[at_chunk(n), :] = 1.0 / inverse[at_chunk(n), :]
        return carry

    lax.fori_loop(0, chunks, invert, 0, unroll=2)

    def first_faces(f, planes):
        face_update(change, PAD, f, face_link[f] * planes)
        face_link[f] = face_link[f] * plane_rows(inverse, PAD, f)

    finish_faces(1, first_faces)

    centre = 0.5 * (UPPER_BOUND + LOWER_BOUND)
    half_width = 0.5 * (UPPER_BOUND - LOWER_BOUND)
    relative = centre / half_width
    ratio = 1.0 / relative

    for part in range(PARTS):
        arrived(part_recv, part, heat_got.at[part, pl.ds(0, (devices - 1) * 2 * PLANES)])

        def place_heat(t, carry, part=part):
            at = rows_of(t + part * PLANES)
            here = field_a[at, :]
            added = placed_16(heat_got, part, t, PLANES) * heat_scale_row
            right[at, :] = MASS_TERM * here + added
            step = (1.0 / centre) * ((change[at, :] + added) * inverse[at, :] - here)
            change[at, :] = step
            field_b[at, :] = here + step
            return carry

        lax.fori_loop(0, PLANES, place_heat, 0, unroll=2)

    now, then = field_b, field_a
    for sweep in range(1, SWEEPS):
        ratio_next = 1.0 / (2.0 * relative - ratio)
        keep, gain = ratio_next * ratio, 2.0 * ratio_next / half_width
        ratio = ratio_next
        start_faces(now, sweep + 1)

        def relax(n, carry, now=now, then=then, keep=keep, gain=gain, sweep=sweep):
            here = now[at_chunk(n), :]
            pulled = right[at_chunk(n), :] + inner_sum(now, n)
            step = gain * (pulled * inverse[at_chunk(n), :] - here) + keep * change[at_chunk(n), :]
            if sweep < SWEEPS - 1:
                change[at_chunk(n), :] = step
            then[at_chunk(n), :] = here + step
            return carry

        lax.fori_loop(0, chunks, relax, 0, unroll=2)

        def add_faces(f, planes, then=then, gain=gain, sweep=sweep):
            added = gain * face_link[f] * planes
            face_update(then, PAD, f, added)
            if sweep < SWEEPS - 1:
                face_update(change, PAD, f, added)

        finish_faces(sweep + 1, add_faces)
        now, then = then, now

    def write_out(t, carry):
        out_ref[:, pl.ds(pl.multiple_of(t * PLANE, PLANE), PLANE)] = now[rows_of(t), :].T
        return carry

    lax.fori_loop(0, B, write_out, 0, unroll=2)

    for round_ in range(SWEEPS + 1):
        for copy in face_copies(round_):
            copy.wait_send()
    arrived(meta_sems, 0, meta_out.at[pl.ds(0, devices - 1)])
    for field in range(2):
        arrived(send_sems, field, words_out.at[field, pl.ds(0, (devices - 1) * 2 * B)])
    for part in range(PARTS):
        arrived(part_send, part, heat_out.at[part, pl.ds(0, (devices - 1) * 2 * PLANES)])


def local(place, warmth, forcing, kappa, depth, tile, side, turn, devices, minor):
    slots = place.shape[0]
    blocks = depth.shape[0]
    lanes = 128
    tall = CELLS + 2 * PAD
    vmem = pl.BlockSpec(memory_space=pltpu.VMEM)
    hbm = pl.BlockSpec(memory_space=pl.ANY)
    tall_field = pltpu.VMEM((tall, lanes), F32)
    return pl.pallas_call(
        functools.partial(kernel, devices, minor),
        out_shape=pltpu.VMEM((blocks, CELLS), F32),
        in_specs=[vmem] * 5 + [hbm] * 3,
        out_specs=vmem,
        scratch_shapes=[
            pltpu.VMEM((slots, CELLS), F32),
            pltpu.VMEM((slots, CELLS), BF16),
            pltpu.VMEM((slots, CELLS), BF16),
            pltpu.VMEM((devices, 1, lanes), F32),
            pltpu.VMEM((devices, 1, lanes), F32),
            pltpu.VMEM((2, devices * 2 * B, lanes), I32),
            pltpu.VMEM((2, devices * 2 * B, lanes), I32),
            pltpu.VMEM((PARTS, devices * 2 * PLANES, lanes), I32),
            pltpu.VMEM((PARTS, devices * 2 * PLANES, lanes), I32),
            pltpu.VMEM((slots, slots), BF16),
            pltpu.VMEM((blocks, 4 * devices), BF16),
            tall_field,
            tall_field,
            tall_field,
            tall_field,
            tall_field,
            tall_field,
            tall_field,
            tall_field,
            tall_field,
            pltpu.VMEM((10 * lanes, 6 * lanes), BF16),
            pltpu.VMEM((6 * lanes, lanes), BF16),
            pltpu.VMEM((6, PLANE, lanes), F32),
            pltpu.VMEM((PLANE, lanes), F32),
            pltpu.VMEM((2, PLANE, 6 * lanes), BF16),
            pltpu.VMEM((PLANE, 6 * lanes), BF16),
            pltpu.VMEM((SWEEPS + 1, PLANE, lanes), BF16),
            pltpu.VMEM((SWEEPS + 1, 4, PLANE, lanes), BF16),
            pltpu.VMEM((6, PLANE, lanes), F32),
            pltpu.VMEM((PLANE, 6 * lanes), F32),
            pltpu.SemaphoreType.DMA((3,)),
            pltpu.SemaphoreType.DMA((2,)),
            pltpu.SemaphoreType.DMA((2,)),
            pltpu.SemaphoreType.DMA((2,)),
            pltpu.SemaphoreType.DMA((PARTS,)),
            pltpu.SemaphoreType.DMA((PARTS,)),
            pltpu.SemaphoreType.DMA((SWEEPS + 1, 4)),
            pltpu.SemaphoreType.DMA((SWEEPS + 1, 4)),
        ],
        compiler_params=pltpu.CompilerParams(
            collective_id=0, has_side_effects=True, vmem_limit_bytes=54 * 2**20
        ),
    )(
        place.reshape(1, slots),
        depth.reshape(1, blocks),
        tile,
        side,
        turn,
        warmth,
        forcing,
        kappa,
    )


def solution(mesh):
    both = ("gx", "gy")
    devices = mesh.shape["gx"] * mesh.shape["gy"]
    return jax.shard_map(
        functools.partial(local, devices=devices, minor=mesh.shape["gy"]),
        mesh=mesh,
        in_specs=(
            P(both),
            P(both, None),
            P(both, None),
            P(both, None),
            P(both),
            P(None, both),
            P(None, both),
            P(None, both),
        ),
        out_specs=P(both, None),
        check_vma=False,
    )
```

```python
import functools

import jax
import jax.numpy as jnp
from jax import lax
from jax.experimental import pallas as pl
from jax.experimental.pallas import tpu as pltpu
from jax.sharding import PartitionSpec as P

B = 16
PLANE = B * B
CELLS = B * B * B
SWEEPS = 3
MASS_TERM = 4.0
LOWER_BOUND = 0.25
UPPER_BOUND = 2.0
CHUNK = 64
PARTS = 8
FACE_CAP = 32
FOLD = PLANE // 4
PLANES = B // PARTS
EARLY = 4
LATE = 6
PAD = PLANE
LEVELS = 32767.0
F32 = jnp.float32
BF16 = jnp.bfloat16
I32 = jnp.int32
MESH = pl.DeviceIdType.MESH


def dot(a, b):
    return jnp.dot(a, b, preferred_element_type=F32)


def plane_rows(ref, base, face):
    if face == 0:
        return ref[pl.ds(base, PLANE), :]
    if face == 1:
        return ref[pl.ds(base + 15 * PLANE, PLANE), :]
    if face in (2, 3):
        first = base + (0 if face == 2 else PLANE - B)
        return jnp.concatenate([ref[pl.ds(first + PLANE * u, B), :] for u in range(B)], axis=0)
    return ref[pl.ds(base + (0 if face == 4 else B - 1), PLANE, stride=B), :]


def crossed_groups(ref, base, face):
    if face < 2:
        first, step, stride = base + 15 * PLANE * face, 1, B
    elif face < 4:
        first, step, stride = base + (PLANE - B) * (face - 2), 1, PLANE
    else:
        first, step, stride = base + (B - 1) * (face - 4), B, PLANE
    return [ref[pl.ds(first + step * v, B, stride=stride), :] for v in range(B)]


def face_update(ref, base, face, added):
    if face < 2:
        at = pl.ds(base + 15 * PLANE * face, PLANE)
        ref[at, :] = ref[at, :] + added
    elif face < 4:
        first = base + (PLANE - B) * (face - 2)
        for u in range(B):
            at = pl.ds(first + PLANE * u, B)
            ref[at, :] = ref[at, :] + added[u * B : (u + 1) * B]
    else:
        at = pl.ds(base + (B - 1) * (face - 4), PLANE, stride=B)
        ref[at, :] = ref[at, :] + added


def harmonic(p, q):
    return 2.0 * p * q / (p + q)


def kernel(
    devices,
    minor,
    place_ref,
    depth_ref,
    tile_ref,
    side_ref,
    turn_ref,
    warm_hbm,
    heat_hbm,
    kappa_hbm,
    out_ref,
    warm_in,
    heat_in,
    kappa_in,
    meta_out,
    meta_got,
    words_out,
    words_got,
    heat_out,
    heat_got,
    onehot,
    settle,
    conduct,
    link_i,
    link_j,
    link_k,
    right,
    inverse,
    field_a,
    field_b,
    change,
    gather,
    choose,
    turned,
    picked,
    high,
    low,
    leaving,
    arriving,
    face_link,
    near,
    load_sem,
    meta_sems,
    send_sems,
    recv_sems,
    part_send,
    part_recv,
    face_send,
    face_recv,
):
    major = devices // minor
    gx = lax.axis_index("gx")
    gy = lax.axis_index("gy")
    me = gx * minor + gy
    slots = place_ref.shape[1]
    lanes = 128
    barrier = pltpu.get_barrier_semaphore()

    def peer(t):
        p = lax.rem(me + t * 37, devices)
        return p, (lax.div(p, minor), lax.rem(p, minor))

    def greet(t, carry):
        pl.semaphore_signal(barrier, inc=1, device_id=peer(t)[1], device_id_type=MESH)
        return carry

    loads = [
        pltpu.make_async_copy(kappa_hbm, kappa_in, load_sem.at[0]),
        pltpu.make_async_copy(warm_hbm, warm_in, load_sem.at[1]),
        pltpu.make_async_copy(heat_hbm, heat_in, load_sem.at[2]),
    ]
    for copy in loads:
        copy.start()
    lax.fori_loop(1, devices, greet, 0)

    place_row = place_ref[...].astype(F32)
    row_id = lax.broadcasted_iota(I32, (slots, slots), 0)
    col_id = lax.broadcasted_iota(I32, (slots, slots), 1)
    place_wide = jnp.broadcast_to(place_row, (slots, slots))
    place_col = jnp.sum(jnp.where(row_id == col_id, place_wide, 0.0), axis=1, keepdims=True)
    owner_row = jnp.floor(place_wide * (1.0 / lanes))
    owner_col = jnp.floor(place_col * (1.0 / lanes))
    again = jnp.sum(
        jnp.where((owner_row == owner_col) & (row_id < col_id), 1.0, 0.0), axis=0, keepdims=True
    )
    row_at = jnp.where(place_row >= 0.0, again * devices + owner_row[:1], -1.0)
    onehot[...] = jnp.where(row_id.astype(F32) == row_at, 1.0, 0.0).astype(BF16)
    tag_col = jnp.where(place_col >= 0.0, place_col - owner_col * lanes + 1.0, 0.0)
    tags = dot(onehot[...], jnp.broadcast_to(tag_col, (slots, lanes)).astype(BF16))

    def put_words(ref, field, t, planes, words):
        for s in range(2):
            ref[field, pl.ds(s * planes + t, devices, stride=2 * planes), :] = words[
                s * devices : (s + 1) * devices
            ]

    def send_words(out, got, field, rows, sem_out, sem_got):
        def block(p):
            return pl.ds(pl.multiple_of(p * rows, rows), rows)

        def one(t, carry):
            p, where = peer(t)
            pltpu.make_async_remote_copy(
                out.at[field, block(p)],
                got.at[field, block(me)],
                sem_out.at[field],
                sem_got.at[field],
                device_id=where,
                device_id_type=MESH,
            ).start()
            return carry

        lax.fori_loop(1, devices, one, 0)
        got[field, block(me), :] = out[field, block(me), :]

    def send_field(field):
        send_words(words_out, words_got, field, 2 * B, send_sems, recv_sems)

    def send_part(part):
        send_words(heat_out, heat_got, part, 2 * PLANES, part_send, part_recv)

    loads[0].wait()

    def pack_kappa(t, carry):
        both = dot(onehot[...], kappa_in[:, pl.ds(pl.multiple_of(t * PLANE, PLANE), PLANE)])
        ints = (both * 256.0).astype(I32)
        put_words(words_out, 0, t, B, ints[:, :lanes] + ints[:, lanes:] * 65536)
        return carry

    lax.fori_loop(0, B, pack_kappa, 0, unroll=2)
    pl.semaphore_wait(barrier, devices - 1)
    send_field(0)

    loads[1].wait()
    loads[2].wait()

    def scale_of(ref):
        def one(t, best):
            at = pl.ds(pl.multiple_of(t * lanes, lanes), lanes)
            return jnp.maximum(best, jnp.abs(ref[:, at].astype(F32)))

        best = lax.fori_loop(0, CELLS // lanes, one, jnp.zeros((slots, lanes), F32))
        largest = jnp.maximum(jnp.max(best, axis=1, keepdims=True) * 1.005, 1e-30)
        return dot(onehot[...], jnp.broadcast_to(largest, (slots, lanes)).astype(BF16))

    warm_scale = scale_of(warm_in)
    heat_scale = scale_of(heat_in)
    lane_id = lax.broadcasted_iota(I32, (devices, lanes), 1)
    meta = jnp.zeros((devices, lanes), F32)
    for n, part in enumerate((tags, warm_scale, heat_scale)):
        for s in range(2):
            meta = jnp.where(lane_id == 2 * n + s, part[s * devices : (s + 1) * devices], meta)
    meta_out[...] = meta.reshape(devices, 1, lanes)
    meta_got[pl.ds(me, 1)] = meta_out[pl.ds(me, 1)]

    def send_meta(t, carry):
        p, where = peer(t)
        pltpu.make_async_remote_copy(
            meta_out.at[p],
            meta_got.at[me],
            meta_sems.at[0],
            meta_sems.at[1],
            device_id=where,
            device_id_type=MESH,
        ).start()
        return carry

    lax.fori_loop(1, devices, send_meta, 0)

    def factor(scale):
        return jnp.where(scale > 0.0, LEVELS / jnp.maximum(scale, 1e-31), 0.0)

    warm_factor = factor(warm_scale)
    heat_factor = factor(heat_scale)

    def words_of(both, scale):
        ints = [jnp.round(both[:, c * lanes : (c + 1) * lanes] * scale).astype(I32) for c in (0, 1)]
        return ints[0] + ints[1] * 65536

    def pack_warm(t, carry):
        value = warm_in[:, pl.ds(pl.multiple_of(t * PLANE, PLANE), PLANE)]
        top = value.astype(BF16)
        rest = (value - top.astype(F32)).astype(BF16)
        both = dot(onehot[...], top) + dot(onehot[...], rest)
        put_words(words_out, 1, t, B, words_of(both, warm_factor))
        return carry

    lax.fori_loop(0, B, pack_warm, 0, unroll=2)
    send_field(1)

    def pack_heat(t, carry):
        both = dot(onehot[...], heat_in[:, pl.ds(pl.multiple_of(t * PLANE, PLANE), PLANE)])
        put_words(heat_out, t // PLANES, t % PLANES, PLANES, words_of(both, heat_factor))
        return carry

    lax.fori_loop(0, B, pack_heat, 0, unroll=2)
    for part in range(EARLY):
        send_part(part)

    swaps, flip_rows, flip_cols, linked = [], [], [], []
    ways = []
    insides = []
    turn_bits = []
    for f in range(6):
        tile = tile_ref[f : f + 1, :]
        turn = turn_ref[f : f + 1, :]
        owner = tile >> 7
        inside = tile & 127
        live = tile >= 0
        way = jnp.where(
            owner == me - minor,
            0,
            jnp.where(owner == me + minor, 1, jnp.where(owner == me - 1, 2, 3)),
        )
        way = jnp.where(owner == me, -1, way)
        way = jnp.where(live, way, -2)
        ways.append(way)
        insides.append(inside)
        swap = turn >> 2
        bit_0 = turn & 1
        bit_1 = (turn >> 1) & 1
        turn_bits.append(
            [swap, jnp.where(swap > 0, bit_1, bit_0), jnp.where(swap > 0, bit_0, bit_1)]
        )
        swaps.append(jnp.broadcast_to(swap, (B, lanes)) > 0)
        flip_rows.append(jnp.broadcast_to(jnp.where(swap > 0, bit_1, bit_0), (B, lanes)) > 0)
        flip_cols.append(jnp.broadcast_to(jnp.where(swap > 0, bit_0, bit_1), (B, lanes)) > 0)
        linked.append(jnp.broadcast_to(tile, (PLANE, lanes)) >= 0)
    square = lax.broadcasted_iota(I32, (lanes, lanes), 0)
    across = lax.broadcasted_iota(I32, (lanes, lanes), 1)
    def column(row):
        return jnp.sum(jnp.where(square == across, row, 0.0), axis=1, keepdims=True)

    def below(counts, limit):
        return jnp.sum(jnp.where(square < limit, counts, 0.0), axis=0, keepdims=True)

    ranks, theirs = [], []
    for d in range(4):
        sends = sum(jnp.where(ways[f] == d, 1.0, 0.0) for f in range(6))
        ranks.append(below(column(sends), across))
        marks = sum(
            jnp.where((square == insides[f]) & (ways[f] == d), 1.0, 0.0) for f in range(6)
        )
        theirs.append(jnp.sum(marks, axis=1, keepdims=True))
    for f in range(6):
        at = pl.ds(f * lanes, lanes)
        source = jnp.where(
            ways[f] == -1, (side_ref[f : f + 1, :] * lanes + insides[f]).astype(F32), -1.0
        )
        lane = jnp.full((1, lanes), -1.0, F32)
        for d in range(4):
            slot = below(theirs[d], insides[f])
            source = jnp.where(ways[f] == d, 6 * lanes + d * FACE_CAP + slot, source)
            lane = jnp.where(ways[f] == d, d * FACE_CAP + ranks[d], lane)
        source = source.astype(I32)
        for n in range(7):
            gather[pl.ds(n * lanes, lanes), at] = jnp.where(
                square + n * lanes == source, 1.0, 0.0
            ).astype(BF16)
        choose[at, :] = jnp.where(column(lane) == across.astype(F32), 1.0, 0.0).astype(BF16)
    sent_bits = [
        jnp.broadcast_to(
            dot(
                jnp.concatenate(
                    [jnp.broadcast_to(turn_bits[f][n], (B, lanes)) for f in range(6)], axis=1
                ).astype(F32).astype(BF16),
                choose[...],
            ),
            (B, lanes),
        )
        > 0.5
        for n in range(3)
    ]
    for ref in (conduct, link_i, link_j, link_k, field_a, field_b):
        fill = jnp.full((PAD, lanes), 1.0 if ref is conduct else 0.0, F32)
        ref[pl.ds(0, PAD), :] = fill
        ref[pl.ds(PAD + CELLS, PAD), :] = fill

    neighbours = (
        (lax.rem(gx + major - 1, major), gy),
        (lax.rem(gx + 1, major), gy),
        (gx, lax.rem(gy + minor - 1, minor)),
        (gx, lax.rem(gy + 1, minor)),
    )

    def face_copies(round_):
        return [
            pltpu.make_async_remote_copy(
                leaving.at[round_, d],
                arriving.at[round_, d ^ 1],
                face_send.at[round_, d],
                face_recv.at[round_, d ^ 1],
                device_id=neighbours[d],
                device_id_type=MESH,
            )
            for d in range(4)
        ]

    def turn_planes(plain, crossed, scratch, swap, flip_col):
        laid = [jnp.where(swap, plain[c * B : (c + 1) * B], crossed[c]) for c in range(B)]
        for c in range(B):
            scratch[pl.ds(c * B, B), :] = jnp.where(flip_col, laid[B - 1 - c], laid[c])

    def turned_back(scratch, flip_row):
        back = [scratch[pl.ds(r, B, stride=B), :] for r in range(B)]
        return jnp.concatenate(
            [jnp.where(flip_row, back[B - 1 - r], back[r]) for r in range(B)], axis=0
        )

    quarter = lax.broadcasted_iota(I32, (FOLD, lanes), 1) >> 5

    def rolled(value, quarters):
        shift = FACE_CAP * quarters % lanes
        return pltpu.roll(value, shift, axis=1) if shift else value

    def start_faces(ref, round_):
        which = min(round_, 1)
        for f in range(6):
            low[:, pl.ds(f * lanes, lanes)] = plane_rows(ref, PAD, f).astype(BF16)
        sent = dot(low[...], choose[...])
        picked[...] = sent
        crossed = [picked[pl.ds(v, B, stride=B), :] for v in range(B)]
        turn_planes(sent, crossed, turned.at[0], sent_bits[0], sent_bits[2])
        plane = turned_back(turned.at[0], sent_bits[1])
        for d in range(4):
            folded = jnp.zeros((FOLD, lanes), F32)
            for q in range(4):
                moved = rolled(plane[q * FOLD : (q + 1) * FOLD], q - d)
                folded = jnp.where(quarter == q, moved, folded)
            leaving[round_, d] = folded.astype(BF16)
        for copy in face_copies(round_):
            copy.start()
        for f in range(6):
            turn_planes(
                plane_rows(ref, PAD, f),
                crossed_groups(ref, PAD, f),
                turned.at[f],
                swaps[f],
                flip_cols[f],
            )
        for f in range(6):
            plane = turned_back(turned.at[f], flip_rows[f])
            top = plane.astype(BF16)
            at = pl.ds(f * lanes, lanes)
            high[which, :, at] = top
            if round_ > 0:
                low[:, at] = (plane - top.astype(F32)).astype(BF16)

    def finish_faces(round_, use):
        for pair in range(3):
            at = pl.ds(pair * 2 * lanes, 2 * lanes)
            planes = dot(high[min(round_, 1)], gather[pl.ds(0, 6 * lanes), at])
            if round_ > 0:
                planes = planes + dot(low[...], gather[pl.ds(0, 6 * lanes), at])
            near[:, at] = planes
        for copy in face_copies(round_):
            copy.wait_recv()
        came = [arriving[round_, d].astype(F32) for d in range(4)]
        unfolded = []
        for q in range(4):
            rows = jnp.zeros((FOLD, lanes), F32)
            for d in range(4):
                rows = jnp.where(quarter == d, rolled(came[d], d - q), rows)
            unfolded.append(rows)
        far = jnp.concatenate(unfolded, axis=0).astype(BF16)
        for pair in range(3):
            at = pl.ds(pair * 2 * lanes, 2 * lanes)
            planes = near[:, at] + dot(far, gather[pl.ds(6 * lanes, lanes), at])
            use(2 * pair, planes[:, :lanes])
            use(2 * pair + 1, planes[:, lanes:])

    def arrived(sems, sem, buffer):
        pltpu.make_async_copy(buffer, buffer, sems.at[sem]).wait()

    def all_but_mine(field):
        return words_got.at[field, pl.ds(0, (devices - 1) * 2 * B)]

    arrived(meta_sems, 1, meta_got.at[pl.ds(0, devices - 1)])
    meta = meta_got[...].reshape(devices, lanes)
    spread = [
        jnp.concatenate(
            [jnp.broadcast_to(meta[:, 2 * n + s : 2 * n + s + 1], (devices, lanes)) for s in range(2)],
            axis=0,
        )
        for n in range(3)
    ]
    block_id = lax.broadcasted_iota(I32, (2 * devices, lanes), 1).astype(F32)
    chosen = jnp.where(spread[0] == block_id + 1.0, 1.0, 0.0)
    warm_unit = jnp.sum(chosen * spread[1], axis=0, keepdims=True) * (1.0 / LEVELS)
    heat_scale_row = jnp.sum(chosen * spread[2], axis=0, keepdims=True) * (MASS_TERM / LEVELS)
    by_block = chosen.T
    settle[:, : 2 * devices] = (by_block * 256.0).astype(BF16)
    settle[:, 2 * devices :] = by_block.astype(BF16)

    def words_at(ref, field, t, planes):
        words = jnp.concatenate(
            [ref[field, pl.ds(s * planes + t, devices, stride=2 * planes), :] for s in range(2)], axis=0
        )
        second = (words + 32768) >> 16
        first = words - second * 65536
        return jnp.concatenate([first, second], axis=1)

    def placed_16(ref, field, t, planes):
        ints = words_at(ref, field, t, planes)
        top = ints >> 8
        rest = ints & 255
        parts = jnp.concatenate([top.astype(F32).astype(BF16), rest.astype(F32).astype(BF16)], axis=0)
        return dot(settle[...], parts).T

    depth = depth_ref[...]
    level = jnp.where(depth == 0, 1.0, jnp.where(depth == 1, 4.0, 16.0)) * (1.0 / 256.0)

    def rows_of(t):
        return pl.ds(pl.multiple_of(PAD + t * PLANE, PLANE), PLANE)

    arrived(recv_sems, 0, all_but_mine(0))

    def place_kappa(t, carry):
        ints = words_at(words_got, 0, t, B).astype(F32).astype(BF16)
        conduct[rows_of(t), :] = dot(settle[:, 2 * devices :], ints).T * level
        return carry

    lax.fori_loop(0, B, place_kappa, 0, unroll=2)
    start_faces(conduct, 0)
    for part in range(EARLY, LATE):
        send_part(part)

    row_in = lax.broadcasted_iota(I32, (CHUNK, lanes), 0)
    inner_k = (row_in & (B - 1)) < B - 1
    chunks = CELLS // CHUNK

    def at_chunk(n, shift=0):
        return pl.ds(pl.multiple_of(PAD + n * CHUNK, CHUNK) + shift, CHUNK)

    def make_links(n, carry):
        here = conduct[at_chunk(n), :]
        row = row_in + n * CHUNK
        link_i[at_chunk(n), :] = jnp.where(
            row < CELLS - PLANE, harmonic(here, conduct[at_chunk(n, PLANE), :]), 0.0
        )
        link_j[at_chunk(n), :] = jnp.where(
            (row & (PLANE - 1)) < PLANE - B, harmonic(here, conduct[at_chunk(n, B), :]), 0.0
        )
        link_k[at_chunk(n), :] = jnp.where(inner_k, harmonic(here, conduct[at_chunk(n, 1), :]), 0.0)
        return carry

    lax.fori_loop(0, chunks, make_links, 0, unroll=2)

    def add_links(n, carry):
        inverse[at_chunk(n), :] = (
            MASS_TERM
            + link_i[at_chunk(n), :]
            + link_i[at_chunk(n, -PLANE), :]
            + link_j[at_chunk(n), :]
            + link_j[at_chunk(n, -B), :]
            + link_k[at_chunk(n), :]
            + link_k[at_chunk(n, -1), :]
        )
        return carry

    lax.fori_loop(0, chunks, add_links, 0, unroll=2)

    arrived(recv_sems, 1, all_but_mine(1))

    def place_warm(t, carry):
        field_a[rows_of(t), :] = placed_16(words_got, 1, t, B) * warm_unit
        return carry

    lax.fori_loop(0, B, place_warm, 0, unroll=2)
    start_faces(field_a, 1)
    for part in range(LATE, PARTS):
        send_part(part)

    def inner_sum(now, n):
        return (
            link_i[at_chunk(n), :] * now[at_chunk(n, PLANE), :]
            + link_i[at_chunk(n, -PLANE), :] * now[at_chunk(n, -PLANE), :]
            + link_j[at_chunk(n), :] * now[at_chunk(n, B), :]
            + link_j[at_chunk(n, -B), :] * now[at_chunk(n, -B), :]
            + link_k[at_chunk(n), :] * now[at_chunk(n, 1), :]
            + link_k[at_chunk(n, -1), :] * now[at_chunk(n, -1), :]
        )

    def first_sum(n, carry):
        change[at_chunk(n), :] = MASS_TERM * field_a[at_chunk(n), :] + inner_sum(field_a, n)
        return carry

    lax.fori_loop(0, chunks, first_sum, 0, unroll=2)

    def make_face_links(f, planes):
        links = jnp.where(
            linked[f], harmonic(plane_rows(conduct, PAD, f), jnp.where(linked[f], planes, 1.0)), 0.0
        )
        face_link[f] = links
        face_update(inverse, PAD, f, links)

    finish_faces(0, make_face_links)

    def invert(n, carry):
        inverse[at_chunk(n), :] = 1.0 / inverse[at_chunk(n), :]
        return carry

    lax.fori_loop(0, chunks, invert, 0, unroll=2)

    def first_faces(f, planes):
        face_update(change, PAD, f, face_link[f] * planes)
        face_link[f] = face_link[f] * plane_rows(inverse, PAD, f)

    finish_faces(1, first_faces)

    centre = 0.5 * (UPPER_BOUND + LOWER_BOUND)
    half_width = 0.5 * (UPPER_BOUND - LOWER_BOUND)
    relative = centre / half_width
    ratio = 1.0 / relative

    for part in range(PARTS):
        arrived(part_recv, part, heat_got.at[part, pl.ds(0, (devices - 1) * 2 * PLANES)])

        def place_heat(t, carry, part=part):
            at = rows_of(t + part * PLANES)
            here = field_a[at, :]
            added = placed_16(heat_got, part, t, PLANES) * heat_scale_row
            right[at, :] = MASS_TERM * here + added
            step = (1.0 / centre) * ((change[at, :] + added) * inverse[at, :] - here)
            change[at, :] = step
            field_b[at, :] = here + step
            return carry

        lax.fori_loop(0, PLANES, place_heat, 0, unroll=2)

    now, then = field_b, field_a
    for sweep in range(1, SWEEPS):
        ratio_next = 1.0 / (2.0 * relative - ratio)
        keep, gain = ratio_next * ratio, 2.0 * ratio_next / half_width
        ratio = ratio_next
        start_faces(now, sweep + 1)
        if sweep > 1:
            for f in range(6):
                face_update(change, PAD, f, near[:, pl.ds(f * lanes, lanes)])

        def relax(n, carry, now=now, then=then, keep=keep, gain=gain, sweep=sweep):
            here = now[at_chunk(n), :]
            pulled = right[at_chunk(n), :] + inner_sum(now, n)
            step = gain * (pulled * inverse[at_chunk(n), :] - here) + keep * change[at_chunk(n), :]
            if sweep < SWEEPS - 1:
                change[at_chunk(n), :] = step
            then[at_chunk(n), :] = here + step
            return carry

        lax.fori_loop(0, chunks, relax, 0, unroll=2)

        def add_faces(f, planes, then=then, gain=gain, sweep=sweep):
            added = gain * face_link[f] * planes
            face_update(then, PAD, f, added)
            if sweep < SWEEPS - 1:
                near[:, pl.ds(f * lanes, lanes)] = added

        finish_faces(sweep + 1, add_faces)
        now, then = then, now

    def write_out(t, carry):
        out_ref[:, pl.ds(pl.multiple_of(t * PLANE, PLANE), PLANE)] = now[rows_of(t), :].T
        return carry

    lax.fori_loop(0, B, write_out, 0, unroll=4)

    for round_ in range(SWEEPS + 1):
        for copy in face_copies(round_):
            copy.wait_send()
    arrived(meta_sems, 0, meta_out.at[pl.ds(0, devices - 1)])
    for field in range(2):
        arrived(send_sems, field, words_out.at[field, pl.ds(0, (devices - 1) * 2 * B)])
    for part in range(PARTS):
        arrived(part_send, part, heat_out.at[part, pl.ds(0, (devices - 1) * 2 * PLANES)])


def local(place, warmth, forcing, kappa, depth, tile, side, turn, devices, minor):
    slots = place.shape[0]
    blocks = depth.shape[0]
    lanes = 128
    tall = CELLS + 2 * PAD
    vmem = pl.BlockSpec(memory_space=pltpu.VMEM)
    hbm = pl.BlockSpec(memory_space=pl.ANY)
    tall_field = pltpu.VMEM((tall, lanes), F32)
    return pl.pallas_call(
        functools.partial(kernel, devices, minor),
        out_shape=pltpu.VMEM((blocks, CELLS), F32),
        in_specs=[vmem] * 5 + [hbm] * 3,
        out_specs=vmem,
        scratch_shapes=[
            pltpu.VMEM((slots, CELLS), F32),
            pltpu.VMEM((slots, CELLS), BF16),
            pltpu.VMEM((slots, CELLS), BF16),
            pltpu.VMEM((devices, 1, lanes), F32),
            pltpu.VMEM((devices, 1, lanes), F32),
            pltpu.VMEM((2, devices * 2 * B, lanes), I32),
            pltpu.VMEM((2, devices * 2 * B, lanes), I32),
            pltpu.VMEM((PARTS, devices * 2 * PLANES, lanes), I32),
            pltpu.VMEM((PARTS, devices * 2 * PLANES, lanes), I32),
            pltpu.VMEM((slots, slots), BF16),
            pltpu.VMEM((blocks, 4 * devices), BF16),
            tall_field,
            tall_field,
            tall_field,
            tall_field,
            tall_field,
            tall_field,
            tall_field,
            tall_field,
            tall_field,
            pltpu.VMEM((7 * lanes, 6 * lanes), BF16),
            pltpu.VMEM((6 * lanes, lanes), BF16),
            pltpu.VMEM((6, PLANE, lanes), F32),
            pltpu.VMEM((PLANE, lanes), F32),
            pltpu.VMEM((2, PLANE, 6 * lanes), BF16),
            pltpu.VMEM((PLANE, 6 * lanes), BF16),
            pltpu.VMEM((SWEEPS + 1, 4, FOLD, lanes), BF16),
            pltpu.VMEM((SWEEPS + 1, 4, FOLD, lanes), BF16),
            pltpu.VMEM((6, PLANE, lanes), F32),
            pltpu.VMEM((PLANE, 6 * lanes), F32),
            pltpu.SemaphoreType.DMA((3,)),
            pltpu.SemaphoreType.DMA((2,)),
            pltpu.SemaphoreType.DMA((2,)),
            pltpu.SemaphoreType.DMA((2,)),
            pltpu.SemaphoreType.DMA((PARTS,)),
            pltpu.SemaphoreType.DMA((PARTS,)),
            pltpu.SemaphoreType.DMA((SWEEPS + 1, 4)),
            pltpu.SemaphoreType.DMA((SWEEPS + 1, 4)),
        ],
        compiler_params=pltpu.CompilerParams(
            collective_id=0, has_side_effects=True, vmem_limit_bytes=54 * 2**20
        ),
    )(
        place.reshape(1, slots),
        depth.reshape(1, blocks),
        tile,
        side,
        turn,
        warmth,
        forcing,
        kappa,
    )


def solution(mesh):
    both = ("gx", "gy")
    devices = mesh.shape["gx"] * mesh.shape["gy"]
    return jax.shard_map(
        functools.partial(local, devices=devices, minor=mesh.shape["gy"]),
        mesh=mesh,
        in_specs=(
            P(both),
            P(both, None),
            P(both, None),
            P(both, None),
            P(both),
            P(None, both),
            P(None, both),
            P(None, both),
        ),
        out_specs=P(both, None),
        check_vma=False,
    )
```

```python
import functools

import jax
import jax.numpy as jnp
from jax import lax
from jax.experimental import pallas as pl
from jax.experimental.pallas import tpu as pltpu
from jax.sharding import PartitionSpec as P

B = 16
PLANE = B * B
CELLS = B * B * B
SWEEPS = 3
MASS_TERM = 4.0
LOWER_BOUND = 0.25
UPPER_BOUND = 2.0
CHUNK = 64
PARTS = 8
FACE_CAP = 32
FOLD = PLANE // 4
PLANES = B // PARTS
EARLY = 4
LATE = 6
PAD = PLANE
LEVELS = 32767.0
F32 = jnp.float32
BF16 = jnp.bfloat16
I32 = jnp.int32
MESH = pl.DeviceIdType.MESH


def dot(a, b):
    return jnp.dot(a, b, preferred_element_type=F32)


def plane_rows(ref, base, face):
    if face == 0:
        return ref[pl.ds(base, PLANE), :]
    if face == 1:
        return ref[pl.ds(base + 15 * PLANE, PLANE), :]
    if face in (2, 3):
        first = base + (0 if face == 2 else PLANE - B)
        return jnp.concatenate([ref[pl.ds(first + PLANE * u, B), :] for u in range(B)], axis=0)
    return ref[pl.ds(base + (0 if face == 4 else B - 1), PLANE, stride=B), :]


def crossed_groups(ref, base, face):
    if face < 2:
        first, step, stride = base + 15 * PLANE * face, 1, B
    elif face < 4:
        first, step, stride = base + (PLANE - B) * (face - 2), 1, PLANE
    else:
        first, step, stride = base + (B - 1) * (face - 4), B, PLANE
    return [ref[pl.ds(first + step * v, B, stride=stride), :] for v in range(B)]


def face_update(ref, base, face, added):
    if face < 2:
        at = pl.ds(base + 15 * PLANE * face, PLANE)
        ref[at, :] = ref[at, :] + added
    elif face < 4:
        first = base + (PLANE - B) * (face - 2)
        for u in range(B):
            at = pl.ds(first + PLANE * u, B)
            ref[at, :] = ref[at, :] + added[u * B : (u + 1) * B]
    else:
        at = pl.ds(base + (B - 1) * (face - 4), PLANE, stride=B)
        ref[at, :] = ref[at, :] + added


def harmonic(p, q):
    return 2.0 * p * q / (p + q)


def kernel(
    devices,
    minor,
    place_ref,
    depth_ref,
    tile_ref,
    side_ref,
    turn_ref,
    warm_hbm,
    heat_hbm,
    kappa_hbm,
    out_ref,
    warm_in,
    heat_in,
    kappa_in,
    meta_out,
    meta_got,
    words_out,
    words_got,
    heat_out,
    heat_got,
    onehot,
    settle,
    conduct,
    link_i,
    link_j,
    link_k,
    right,
    inverse,
    field_a,
    field_b,
    change,
    gather,
    choose,
    turned,
    picked,
    high,
    low,
    leaving,
    arriving,
    face_link,
    near,
    load_sem,
    meta_sems,
    send_sems,
    recv_sems,
    part_send,
    part_recv,
    face_send,
    face_recv,
):
    major = devices // minor
    gx = lax.axis_index("gx")
    gy = lax.axis_index("gy")
    me = gx * minor + gy
    slots = place_ref.shape[1]
    lanes = 128
    barrier = pltpu.get_barrier_semaphore()

    def peer(t):
        p = lax.rem(me + t * 85, devices)
        return p, (lax.div(p, minor), lax.rem(p, minor))

    def greet(t, carry):
        pl.semaphore_signal(barrier, inc=1, device_id=peer(t)[1], device_id_type=MESH)
        return carry

    loads = [
        pltpu.make_async_copy(kappa_hbm, kappa_in, load_sem.at[0]),
        pltpu.make_async_copy(warm_hbm, warm_in, load_sem.at[1]),
        pltpu.make_async_copy(heat_hbm, heat_in, load_sem.at[2]),
    ]
    for copy in loads:
        copy.start()
    lax.fori_loop(1, devices, greet, 0)

    place_row = place_ref[...].astype(F32)
    row_id = lax.broadcasted_iota(I32, (slots, slots), 0)
    col_id = lax.broadcasted_iota(I32, (slots, slots), 1)
    place_wide = jnp.broadcast_to(place_row, (slots, slots))
    place_col = jnp.sum(jnp.where(row_id == col_id, place_wide, 0.0), axis=1, keepdims=True)
    owner_row = jnp.floor(place_wide * (1.0 / lanes))
    owner_col = jnp.floor(place_col * (1.0 / lanes))
    again = jnp.sum(
        jnp.where((owner_row == owner_col) & (row_id < col_id), 1.0, 0.0), axis=0, keepdims=True
    )
    row_at = jnp.where(place_row >= 0.0, again * devices + owner_row[:1], -1.0)
    onehot[...] = jnp.where(row_id.astype(F32) == row_at, 1.0, 0.0).astype(BF16)
    tag_col = jnp.where(place_col >= 0.0, place_col - owner_col * lanes + 1.0, 0.0)
    tags = dot(onehot[...], jnp.broadcast_to(tag_col, (slots, lanes)).astype(BF16))

    def put_words(ref, field, t, planes, words):
        for s in range(2):
            ref[field, pl.ds(s * planes + t, devices, stride=2 * planes), :] = words[
                s * devices : (s + 1) * devices
            ]

    def send_words(out, got, field, rows, sem_out, sem_got):
        def block(p):
            return pl.ds(pl.multiple_of(p * rows, rows), rows)

        def one(t, carry):
            p, where = peer(t)
            pltpu.make_async_remote_copy(
                out.at[field, block(p)],
                got.at[field, block(me)],
                sem_out.at[field],
                sem_got.at[field],
                device_id=where,
                device_id_type=MESH,
            ).start()
            return carry

        lax.fori_loop(1, devices, one, 0)
        got[field, block(me), :] = out[field, block(me), :]

    def send_field(field):
        send_words(words_out, words_got, field, 2 * B, send_sems, recv_sems)

    def send_part(part):
        send_words(heat_out, heat_got, part, 2 * PLANES, part_send, part_recv)

    loads[0].wait()

    def pack_kappa(t, carry):
        both = dot(onehot[...], kappa_in[:, pl.ds(pl.multiple_of(t * PLANE, PLANE), PLANE)])
        ints = (both * 256.0).astype(I32)
        put_words(words_out, 0, t, B, ints[:, :lanes] + ints[:, lanes:] * 65536)
        return carry

    lax.fori_loop(0, B, pack_kappa, 0, unroll=2)
    pl.semaphore_wait(barrier, devices - 1)
    send_field(0)

    loads[1].wait()
    loads[2].wait()

    def scale_of(ref):
        def one(t, best):
            at = pl.ds(pl.multiple_of(t * lanes, lanes), lanes)
            return jnp.maximum(best, jnp.abs(ref[:, at].astype(F32)))

        best = lax.fori_loop(0, CELLS // lanes, one, jnp.zeros((slots, lanes), F32))
        largest = jnp.maximum(jnp.max(best, axis=1, keepdims=True) * 1.005, 1e-30)
        return dot(onehot[...], jnp.broadcast_to(largest, (slots, lanes)).astype(BF16))

    warm_scale = scale_of(warm_in)
    heat_scale = scale_of(heat_in)
    lane_id = lax.broadcasted_iota(I32, (devices, lanes), 1)
    meta = jnp.zeros((devices, lanes), F32)
    for n, part in enumerate((tags, warm_scale, heat_scale)):
        for s in range(2):
            meta = jnp.where(lane_id == 2 * n + s, part[s * devices : (s + 1) * devices], meta)
    meta_out[...] = meta.reshape(devices, 1, lanes)
    meta_got[pl.ds(me, 1)] = meta_out[pl.ds(me, 1)]

    def send_meta(t, carry):
        p, where = peer(t)
        pltpu.make_async_remote_copy(
            meta_out.at[p],
            meta_got.at[me],
            meta_sems.at[0],
            meta_sems.at[1],
            device_id=where,
            device_id_type=MESH,
        ).start()
        return carry

    lax.fori_loop(1, devices, send_meta, 0)

    def factor(scale):
        return jnp.where(scale > 0.0, LEVELS / jnp.maximum(scale, 1e-31), 0.0)

    warm_factor = factor(warm_scale)
    heat_factor = factor(heat_scale)

    def words_of(both, scale):
        ints = [jnp.round(both[:, c * lanes : (c + 1) * lanes] * scale).astype(I32) for c in (0, 1)]
        return ints[0] + ints[1] * 65536

    def pack_warm(t, carry):
        value = warm_in[:, pl.ds(pl.multiple_of(t * PLANE, PLANE), PLANE)]
        top = value.astype(BF16)
        rest = (value - top.astype(F32)).astype(BF16)
        both = dot(onehot[...], top) + dot(onehot[...], rest)
        put_words(words_out, 1, t, B, words_of(both, warm_factor))
        return carry

    lax.fori_loop(0, B, pack_warm, 0, unroll=2)
    send_field(1)

    def pack_heat(t, carry):
        both = dot(onehot[...], heat_in[:, pl.ds(pl.multiple_of(t * PLANE, PLANE), PLANE)])
        put_words(heat_out, t // PLANES, t % PLANES, PLANES, words_of(both, heat_factor))
        return carry

    lax.fori_loop(0, B, pack_heat, 0, unroll=2)
    for part in range(EARLY):
        send_part(part)

    swaps, flip_rows, flip_cols, linked = [], [], [], []
    ways = []
    insides = []
    turn_bits = []
    for f in range(6):
        tile = tile_ref[f : f + 1, :]
        turn = turn_ref[f : f + 1, :]
        owner = tile >> 7
        inside = tile & 127
        live = tile >= 0
        way = jnp.where(
            owner == me - minor,
            0,
            jnp.where(owner == me + minor, 1, jnp.where(owner == me - 1, 2, 3)),
        )
        way = jnp.where(owner == me, -1, way)
        way = jnp.where(live, way, -2)
        ways.append(way)
        insides.append(inside)
        swap = turn >> 2
        bit_0 = turn & 1
        bit_1 = (turn >> 1) & 1
        turn_bits.append(
            [swap, jnp.where(swap > 0, bit_1, bit_0), jnp.where(swap > 0, bit_0, bit_1)]
        )
        swaps.append(jnp.broadcast_to(swap, (B, lanes)) > 0)
        flip_rows.append(jnp.broadcast_to(jnp.where(swap > 0, bit_1, bit_0), (B, lanes)) > 0)
        flip_cols.append(jnp.broadcast_to(jnp.where(swap > 0, bit_0, bit_1), (B, lanes)) > 0)
        linked.append(jnp.broadcast_to(tile, (PLANE, lanes)) >= 0)
    square = lax.broadcasted_iota(I32, (lanes, lanes), 0)
    across = lax.broadcasted_iota(I32, (lanes, lanes), 1)
    def column(row):
        return jnp.sum(jnp.where(square == across, row, 0.0), axis=1, keepdims=True)

    def below(counts, limit):
        return jnp.sum(jnp.where(square < limit, counts, 0.0), axis=0, keepdims=True)

    ranks, theirs = [], []
    for d in range(4):
        sends = sum(jnp.where(ways[f] == d, 1.0, 0.0) for f in range(6))
        ranks.append(below(column(sends), across))
        marks = sum(
            jnp.where((square == insides[f]) & (ways[f] == d), 1.0, 0.0) for f in range(6)
        )
        theirs.append(jnp.sum(marks, axis=1, keepdims=True))
    for f in range(6):
        at = pl.ds(f * lanes, lanes)
        source = jnp.where(
            ways[f] == -1, (side_ref[f : f + 1, :] * lanes + insides[f]).astype(F32), -1.0
        )
        lane = jnp.full((1, lanes), -1.0, F32)
        for d in range(4):
            slot = below(theirs[d], insides[f])
            source = jnp.where(ways[f] == d, 6 * lanes + d * FACE_CAP + slot, source)
            lane = jnp.where(ways[f] == d, d * FACE_CAP + ranks[d], lane)
        source = source.astype(I32)
        for n in range(7):
            gather[pl.ds(n * lanes, lanes), at] = jnp.where(
                square + n * lanes == source, 1.0, 0.0
            ).astype(BF16)
        choose[at, :] = jnp.where(column(lane) == across.astype(F32), 1.0, 0.0).astype(BF16)
    sent_bits = [
        jnp.broadcast_to(
            dot(
                jnp.concatenate(
                    [jnp.broadcast_to(turn_bits[f][n], (B, lanes)) for f in range(6)], axis=1
                ).astype(F32).astype(BF16),
                choose[...],
            ),
            (B, lanes),
        )
        > 0.5
        for n in range(3)
    ]
    for ref in (conduct, link_i, link_j, link_k, field_a, field_b):
        fill = jnp.full((PAD, lanes), 1.0 if ref is conduct else 0.0, F32)
        ref[pl.ds(0, PAD), :] = fill
        ref[pl.ds(PAD + CELLS, PAD), :] = fill

    neighbours = (
        (lax.rem(gx + major - 1, major), gy),
        (lax.rem(gx + 1, major), gy),
        (gx, lax.rem(gy + minor - 1, minor)),
        (gx, lax.rem(gy + 1, minor)),
    )

    def face_copies(round_):
        return [
            pltpu.make_async_remote_copy(
                leaving.at[round_, d],
                arriving.at[round_, d ^ 1],
                face_send.at[round_, d],
                face_recv.at[round_, d ^ 1],
                device_id=neighbours[d],
                device_id_type=MESH,
            )
            for d in range(4)
        ]

    def turn_planes(plain, crossed, scratch, swap, flip_col):
        laid = [jnp.where(swap, plain[c * B : (c + 1) * B], crossed[c]) for c in range(B)]
        for c in range(B):
            scratch[pl.ds(c * B, B), :] = jnp.where(flip_col, laid[B - 1 - c], laid[c])

    def turned_back(scratch, flip_row):
        back = [scratch[pl.ds(r, B, stride=B), :] for r in range(B)]
        return jnp.concatenate(
            [jnp.where(flip_row, back[B - 1 - r], back[r]) for r in range(B)], axis=0
        )

    quarter = lax.broadcasted_iota(I32, (FOLD, lanes), 1) >> 5

    def rolled(value, quarters):
        shift = FACE_CAP * quarters % lanes
        return pltpu.roll(value, shift, axis=1) if shift else value

    def start_faces(ref, round_):
        which = min(round_, 1)
        for f in range(6):
            low[:, pl.ds(f * lanes, lanes)] = plane_rows(ref, PAD, f).astype(BF16)
        sent = dot(low[...], choose[...])
        picked[...] = sent
        crossed = [picked[pl.ds(v, B, stride=B), :] for v in range(B)]
        turn_planes(sent, crossed, turned.at[0], sent_bits[0], sent_bits[2])
        plane = turned_back(turned.at[0], sent_bits[1])
        for d in range(4):
            folded = jnp.zeros((FOLD, lanes), F32)
            for q in range(4):
                moved = rolled(plane[q * FOLD : (q + 1) * FOLD], q - d)
                folded = jnp.where(quarter == q, moved, folded)
            leaving[round_, d] = folded.astype(BF16)
        for copy in face_copies(round_):
            copy.start()
        for f in range(6):
            turn_planes(
                plane_rows(ref, PAD, f),
                crossed_groups(ref, PAD, f),
                turned.at[f],
                swaps[f],
                flip_cols[f],
            )
        for f in range(6):
            plane = turned_back(turned.at[f], flip_rows[f])
            top = plane.astype(BF16)
            at = pl.ds(f * lanes, lanes)
            high[which, :, at] = top
            if round_ > 0:
                low[:, at] = (plane - top.astype(F32)).astype(BF16)

    def finish_faces(round_, use):
        for pair in range(3):
            at = pl.ds(pair * 2 * lanes, 2 * lanes)
            planes = dot(high[min(round_, 1)], gather[pl.ds(0, 6 * lanes), at])
            if round_ > 0:
                planes = planes + dot(low[...], gather[pl.ds(0, 6 * lanes), at])
            near[:, at] = planes
        for copy in face_copies(round_):
            copy.wait_recv()
        came = [arriving[round_, d].astype(F32) for d in range(4)]
        unfolded = []
        for q in range(4):
            rows = jnp.zeros((FOLD, lanes), F32)
            for d in range(4):
                rows = jnp.where(quarter == d, rolled(came[d], d - q), rows)
            unfolded.append(rows)
        far = jnp.concatenate(unfolded, axis=0).astype(BF16)
        for pair in range(3):
            at = pl.ds(pair * 2 * lanes, 2 * lanes)
            planes = near[:, at] + dot(far, gather[pl.ds(6 * lanes, lanes), at])
            use(2 * pair, planes[:, :lanes])
            use(2 * pair + 1, planes[:, lanes:])

    def arrived(sems, sem, buffer):
        pltpu.make_async_copy(buffer, buffer, sems.at[sem]).wait()

    def all_but_mine(field):
        return words_got.at[field, pl.ds(0, (devices - 1) * 2 * B)]

    arrived(meta_sems, 1, meta_got.at[pl.ds(0, devices - 1)])
    meta = meta_got[...].reshape(devices, lanes)
    spread = [
        jnp.concatenate(
            [jnp.broadcast_to(meta[:, 2 * n + s : 2 * n + s + 1], (devices, lanes)) for s in range(2)],
            axis=0,
        )
        for n in range(3)
    ]
    block_id = lax.broadcasted_iota(I32, (2 * devices, lanes), 1).astype(F32)
    chosen = jnp.where(spread[0] == block_id + 1.0, 1.0, 0.0)
    warm_unit = jnp.sum(chosen * spread[1], axis=0, keepdims=True) * (1.0 / LEVELS)
    heat_scale_row = jnp.sum(chosen * spread[2], axis=0, keepdims=True) * (MASS_TERM / LEVELS)
    by_block = chosen.T
    settle[:, : 2 * devices] = (by_block * 256.0).astype(BF16)
    settle[:, 2 * devices :] = by_block.astype(BF16)

    def words_at(ref, field, t, planes):
        words = jnp.concatenate(
            [ref[field, pl.ds(s * planes + t, devices, stride=2 * planes), :] for s in range(2)], axis=0
        )
        second = (words + 32768) >> 16
        first = words - second * 65536
        return jnp.concatenate([first, second], axis=1)

    def placed_16(ref, field, t, planes):
        ints = words_at(ref, field, t, planes)
        top = ints >> 8
        rest = ints & 255
        parts = jnp.concatenate([top.astype(F32).astype(BF16), rest.astype(F32).astype(BF16)], axis=0)
        return dot(settle[...], parts).T

    depth = depth_ref[...]
    level = jnp.where(depth == 0, 1.0, jnp.where(depth == 1, 4.0, 16.0)) * (1.0 / 256.0)

    def rows_of(t):
        return pl.ds(pl.multiple_of(PAD + t * PLANE, PLANE), PLANE)

    arrived(recv_sems, 0, all_but_mine(0))

    def place_kappa(t, carry):
        ints = words_at(words_got, 0, t, B).astype(F32).astype(BF16)
        conduct[rows_of(t), :] = dot(settle[:, 2 * devices :], ints).T * level
        return carry

    lax.fori_loop(0, B, place_kappa, 0, unroll=2)
    start_faces(conduct, 0)
    for part in range(EARLY, LATE):
        send_part(part)

    row_in = lax.broadcasted_iota(I32, (CHUNK, lanes), 0)
    inner_k = (row_in & (B - 1)) < B - 1
    chunks = CELLS // CHUNK

    def at_chunk(n, shift=0):
        return pl.ds(pl.multiple_of(PAD + n * CHUNK, CHUNK) + shift, CHUNK)

    def make_links(n, carry):
        here = conduct[at_chunk(n), :]
        row = row_in + n * CHUNK
        link_i[at_chunk(n), :] = jnp.where(
            row < CELLS - PLANE, harmonic(here, conduct[at_chunk(n, PLANE), :]), 0.0
        )
        link_j[at_chunk(n), :] = jnp.where(
            (row & (PLANE - 1)) < PLANE - B, harmonic(here, conduct[at_chunk(n, B), :]), 0.0
        )
        link_k[at_chunk(n), :] = jnp.where(inner_k, harmonic(here, conduct[at_chunk(n, 1), :]), 0.0)
        return carry

    lax.fori_loop(0, chunks, make_links, 0, unroll=2)

    def add_links(n, carry):
        inverse[at_chunk(n), :] = (
            MASS_TERM
            + link_i[at_chunk(n), :]
            + link_i[at_chunk(n, -PLANE), :]
            + link_j[at_chunk(n), :]
            + link_j[at_chunk(n, -B), :]
            + link_k[at_chunk(n), :]
            + link_k[at_chunk(n, -1), :]
        )
        return carry

    lax.fori_loop(0, chunks, add_links, 0, unroll=2)

    arrived(recv_sems, 1, all_but_mine(1))

    def place_warm(t, carry):
        field_a[rows_of(t), :] = placed_16(words_got, 1, t, B) * warm_unit
        return carry

    lax.fori_loop(0, B, place_warm, 0, unroll=2)
    start_faces(field_a, 1)
    for part in range(LATE, PARTS):
        send_part(part)

    def inner_sum(now, n):
        return (
            link_i[at_chunk(n), :] * now[at_chunk(n, PLANE), :]
            + link_i[at_chunk(n, -PLANE), :] * now[at_chunk(n, -PLANE), :]
            + link_j[at_chunk(n), :] * now[at_chunk(n, B), :]
            + link_j[at_chunk(n, -B), :] * now[at_chunk(n, -B), :]
            + link_k[at_chunk(n), :] * now[at_chunk(n, 1), :]
            + link_k[at_chunk(n, -1), :] * now[at_chunk(n, -1), :]
        )

    def first_sum(n, carry):
        change[at_chunk(n), :] = MASS_TERM * field_a[at_chunk(n), :] + inner_sum(field_a, n)
        return carry

    lax.fori_loop(0, chunks, first_sum, 0, unroll=2)

    def make_face_links(f, planes):
        links = jnp.where(
            linked[f], harmonic(plane_rows(conduct, PAD, f), jnp.where(linked[f], planes, 1.0)), 0.0
        )
        face_link[f] = links
        face_update(inverse, PAD, f, links)

    finish_faces(0, make_face_links)

    def invert(n, carry):
        inverse[at_chunk(n), :] = 1.0 / inverse[at_chunk(n), :]
        return carry

    lax.fori_loop(0, chunks, invert, 0, unroll=2)

    def first_faces(f, planes):
        face_update(change, PAD, f, face_link[f] * planes)
        face_link[f] = face_link[f] * plane_rows(inverse, PAD, f)

    finish_faces(1, first_faces)

    centre = 0.5 * (UPPER_BOUND + LOWER_BOUND)
    half_width = 0.5 * (UPPER_BOUND - LOWER_BOUND)
    relative = centre / half_width
    ratio = 1.0 / relative

    for part in range(PARTS):
        arrived(part_recv, part, heat_got.at[part, pl.ds(0, (devices - 1) * 2 * PLANES)])

        def place_heat(t, carry, part=part):
            at = rows_of(t + part * PLANES)
            here = field_a[at, :]
            added = placed_16(heat_got, part, t, PLANES) * heat_scale_row
            right[at, :] = MASS_TERM * here + added
            step = (1.0 / centre) * ((change[at, :] + added) * inverse[at, :] - here)
            change[at, :] = step
            field_b[at, :] = here + step
            return carry

        lax.fori_loop(0, PLANES, place_heat, 0, unroll=2)

    now, then = field_b, field_a
    for sweep in range(1, SWEEPS):
        ratio_next = 1.0 / (2.0 * relative - ratio)
        keep, gain = ratio_next * ratio, 2.0 * ratio_next / half_width
        ratio = ratio_next
        start_faces(now, sweep + 1)
        if sweep > 1:
            for f in range(6):
                face_update(change, PAD, f, near[:, pl.ds(f * lanes, lanes)])

        def relax(n, carry, now=now, then=then, keep=keep, gain=gain, sweep=sweep):
            here = now[at_chunk(n), :]
            pulled = right[at_chunk(n), :] + inner_sum(now, n)
            step = gain * (pulled * inverse[at_chunk(n), :] - here) + keep * change[at_chunk(n), :]
            if sweep < SWEEPS - 1:
                change[at_chunk(n), :] = step
            then[at_chunk(n), :] = here + step
            return carry

        lax.fori_loop(0, chunks, relax, 0, unroll=2)

        def add_faces(f, planes, then=then, gain=gain, sweep=sweep):
            added = gain * face_link[f] * planes
            face_update(then, PAD, f, added)
            if sweep < SWEEPS - 1:
                near[:, pl.ds(f * lanes, lanes)] = added

        finish_faces(sweep + 1, add_faces)
        now, then = then, now

    def write_out(t, carry):
        out_ref[:, pl.ds(pl.multiple_of(t * PLANE, PLANE), PLANE)] = now[rows_of(t), :].T
        return carry

    lax.fori_loop(0, B, write_out, 0, unroll=4)

    for round_ in range(SWEEPS + 1):
        for copy in face_copies(round_):
            copy.wait_send()
    arrived(meta_sems, 0, meta_out.at[pl.ds(0, devices - 1)])
    for field in range(2):
        arrived(send_sems, field, words_out.at[field, pl.ds(0, (devices - 1) * 2 * B)])
    for part in range(PARTS):
        arrived(part_send, part, heat_out.at[part, pl.ds(0, (devices - 1) * 2 * PLANES)])


def local(place, warmth, forcing, kappa, depth, tile, side, turn, devices, minor):
    slots = place.shape[0]
    blocks = depth.shape[0]
    lanes = 128
    tall = CELLS + 2 * PAD
    vmem = pl.BlockSpec(memory_space=pltpu.VMEM)
    hbm = pl.BlockSpec(memory_space=pl.ANY)
    tall_field = pltpu.VMEM((tall, lanes), F32)
    return pl.pallas_call(
        functools.partial(kernel, devices, minor),
        out_shape=pltpu.VMEM((blocks, CELLS), F32),
        in_specs=[vmem] * 5 + [hbm] * 3,
        out_specs=vmem,
        scratch_shapes=[
            pltpu.VMEM((slots, CELLS), F32),
            pltpu.VMEM((slots, CELLS), BF16),
            pltpu.VMEM((slots, CELLS), BF16),
            pltpu.VMEM((devices, 1, lanes), F32),
            pltpu.VMEM((devices, 1, lanes), F32),
            pltpu.VMEM((2, devices * 2 * B, lanes), I32),
            pltpu.VMEM((2, devices * 2 * B, lanes), I32),
            pltpu.VMEM((PARTS, devices * 2 * PLANES, lanes), I32),
            pltpu.VMEM((PARTS, devices * 2 * PLANES, lanes), I32),
            pltpu.VMEM((slots, slots), BF16),
            pltpu.VMEM((blocks, 4 * devices), BF16),
            tall_field,
            tall_field,
            tall_field,
            tall_field,
            tall_field,
            tall_field,
            tall_field,
            tall_field,
            tall_field,
            pltpu.VMEM((7 * lanes, 6 * lanes), BF16),
            pltpu.VMEM((6 * lanes, lanes), BF16),
            pltpu.VMEM((6, PLANE, lanes), F32),
            pltpu.VMEM((PLANE, lanes), F32),
            pltpu.VMEM((2, PLANE, 6 * lanes), BF16),
            pltpu.VMEM((PLANE, 6 * lanes), BF16),
            pltpu.VMEM((SWEEPS + 1, 4, FOLD, lanes), BF16),
            pltpu.VMEM((SWEEPS + 1, 4, FOLD, lanes), BF16),
            pltpu.VMEM((6, PLANE, lanes), F32),
            pltpu.VMEM((PLANE, 6 * lanes), F32),
            pltpu.SemaphoreType.DMA((3,)),
            pltpu.SemaphoreType.DMA((2,)),
            pltpu.SemaphoreType.DMA((2,)),
            pltpu.SemaphoreType.DMA((2,)),
            pltpu.SemaphoreType.DMA((PARTS,)),
            pltpu.SemaphoreType.DMA((PARTS,)),
            pltpu.SemaphoreType.DMA((SWEEPS + 1, 4)),
            pltpu.SemaphoreType.DMA((SWEEPS + 1, 4)),
        ],
        compiler_params=pltpu.CompilerParams(
            collective_id=0, has_side_effects=True, vmem_limit_bytes=54 * 2**20
        ),
    )(
        place.reshape(1, slots),
        depth.reshape(1, blocks),
        tile,
        side,
        turn,
        warmth,
        forcing,
        kappa,
    )


def solution(mesh):
    both = ("gx", "gy")
    devices = mesh.shape["gx"] * mesh.shape["gy"]
    return jax.shard_map(
        functools.partial(local, devices=devices, minor=mesh.shape["gy"]),
        mesh=mesh,
        in_specs=(
            P(both),
            P(both, None),
            P(both, None),
            P(both, None),
            P(both),
            P(None, both),
            P(None, both),
            P(None, both),
        ),
        out_specs=P(both, None),
        check_vma=False,
    )
```
